32 devices in a mesh: grp: 4 (over y, core), sub: 8 (over z, x).
Axes of the slice: x: 2, y: 2, z: 4, core: 2. Of those that a mesh axis runs over, the one named last changes fastest.
Arguments:
- sources: float32 [32, 64, 4096], P(None, None, ('grp', 'sub')), may hold values from -6 to 6
- coords: float32 [3, 64, 4096], P(None, None, ('grp', 'sub')), may hold values from 0 to 2
- leaf_basis: float32 [32, 64, 4096], P(None, None, ('grp', 'sub')), may hold values from -0.75 to 0.75
- transfer: float32 [32, 32, 4096], P(None, None, ('grp', 'sub')), may hold values from -1 to 1
- send_list: int32 [256, 16], P(('grp', 'sub')), may hold values from 0 to 127
- near_list: int32 [7, 4096], P(None, ('grp', 'sub')), may hold values from 0 to 255
- near_count: int32 [4096], P(('grp', 'sub')), may hold values from 1 to 7, as said below
- far_list: int32 [16, 512], P(None, ('grp', 'sub')), may hold values from 0 to 127
- coupling: float32 [32, 32, 16, 512], P(None, None, None, ('grp', 'sub')), may hold values from -0.25 to 0.25
- group_transfer: float32 [32, 32, 512], P(None, None, ('grp', 'sub')), may hold values from -0.09375 to 0.09375
- group_coupling: float32 [32, 32, 4, 4], replicated, may hold values from -1 to 1
Outputs:
- potential: float32 [32, 64, 4096], P(None, None, ('grp', 'sub'))
The draws below stay inside these ranges and needn't reach their ends.
Inputs may be any that keep to these rules, and one draw needn't show every extreme that they name: `near_count`: every device holds a leaf with 7 live entries; the fewest live entries differ from device to device.
All inputs are finite; a program needn't handle non-finite values.
Results may differ from the reference program's by a relative error of at most 0.0003.
Values sent between devices are 32-bit elements; how exact they have to be, the bound alone decides.
A program may use at most 192 MiB of HBM per device.

```python
import math
import jax
import jax.numpy as jnp
from jax import lax

LEAF = 64
RHS = 32
RANK = 32
NEAR = 7
FAR = 16
LEAF_DEV = 128
CAP = 16
SLOTS = 256
PAR_GRP = 128
LEAVES = 4096
PARENTS = 512
N_GRP = 4
N_SUB = 8
DEVICES = 32


def draw_near_count(key, part):
    devices = LEAVES // LEAF_DEV
    first_key = jax.random.fold_in(key, 11)
    second_key = jax.random.fold_in(key, 12)
    lowest = jax.random.randint(first_key, (devices, 1), 1, NEAR)
    counts = jax.random.randint(second_key, (devices, LEAF_DEV), lowest, NEAR + 1)
    counts = counts.at[:, 0].set(NEAR)
    return counts.reshape(-1).astype(jnp.int32)


def set_ends(result, own_key, low, top_value):
    index_at = [jax.random.randint(jax.random.fold_in(own_key, axis), (), 0, length) for axis, length in enumerate(result.shape)]
    widest = result.shape.index(max(result.shape))
    neighbour = index_at[:widest] + [(index_at[widest] + 1) % result.shape[widest]] + index_at[widest + 1:]
    return result.at[tuple(index_at)].set(low).at[tuple(neighbour)].set(top_value)


def block_levels(rng, shape, cuts, smallest, largest):
    gain, own = 1.0, jax.random.fold_in(rng, 6)
    for dim, blocks in cuts:
        heights = jnp.exp(jax.random.uniform(jax.random.fold_in(own, dim), (blocks,), jnp.float32, smallest / len(cuts), largest / len(cuts)))
        gain = gain * jnp.repeat(heights, shape[dim] // blocks).reshape([-1 if axis == dim else 1 for axis in range(len(shape))])
    return gain


def bell_draw(key, extent, scale, bound, cuts=(), kind=jnp.bfloat16):
    values = scale * jax.random.normal(key, extent, jnp.float32)
    if cuts:
        values = values * block_levels(key, extent, cuts, -0.22, 0.18)
    return jnp.clip(values, -bound, bound).astype(kind)


def setup_inputs(seed: int = 0) -> dict:
    keys = jax.random.split(jax.random.key(seed), 12)
    sources = bell_draw(keys[0], (RHS, LEAF, LEAVES), 1.0, 6.0, ((2, 32),), jnp.float32)
    coords = jnp.clip(2.0 * jax.random.uniform(keys[1], (3, LEAF, LEAVES), jnp.float32) ** block_levels(keys[1], (3, LEAF, LEAVES), ((2, 32),), -0.2, 0.2), 0.0, 2.0)
    leaf_basis = bell_draw(keys[2], (RANK, LEAF, LEAVES), LEAF ** -0.5, 0.75, ((2, 32),), jnp.float32)
    transfer = bell_draw(keys[3], (RANK, RANK, LEAVES), RANK ** -0.5, 1.0, ((2, 32),), jnp.float32)
    send_list = set_ends(jax.random.randint(keys[4], (DEVICES * N_SUB, CAP), 0, LEAF_DEV), jax.random.fold_in(keys[4], 1), 0, LEAF_DEV - 1).astype(jnp.int32)
    near_list = set_ends(jax.random.randint(keys[5], (NEAR, LEAVES), 0, SLOTS), jax.random.fold_in(keys[5], 1), 0, SLOTS - 1).astype(jnp.int32)
    near_count = draw_near_count(jax.random.fold_in(keys[11], 71), 0)
    far_list = set_ends(jax.random.randint(keys[7], (FAR, PARENTS), 0, PAR_GRP), jax.random.fold_in(keys[7], 1), 0, PAR_GRP - 1).astype(jnp.int32)
    coupling = bell_draw(keys[8], (RANK, RANK, FAR, PARENTS), (RANK * FAR) ** -0.5, 0.25, ((3, 32),), jnp.float32)
    group_transfer = bell_draw(keys[9], (RANK, RANK, PARENTS), (RANK * PAR_GRP) ** -0.5, 0.09375, ((2, 32),), jnp.float32)
    group_coupling = bell_draw(keys[10], (RANK, RANK, N_GRP, N_GRP), RANK ** -0.5, 1.0, (), jnp.float32)
    return dict(sources=sources, coords=coords, leaf_basis=leaf_basis, transfer=transfer, send_list=send_list, near_list=near_list, near_count=near_count, far_list=far_list, coupling=coupling, group_transfer=group_transfer, group_coupling=group_coupling)


INV_FOUR_PI = 1.0 / (4.0 * math.pi)
EPS_SQ = 0.01
HIGH = lax.Precision.HIGHEST

def near_block(targets, source_pts, source_vals, live):
    offsets = targets[:, :, None, :] - source_pts[:, None, :, :]
    dist_sq = lax.optimization_barrier(jnp.sum(offsets * offsets, axis=0))
    kernel = live.astype(jnp.float32)[None, None, :] * INV_FOUR_PI / jnp.sqrt(dist_sq + EPS_SQ)
    return jnp.einsum('tsl,rsl->rtl', kernel, source_vals, precision=HIGH)

def reference(sources, coords, leaf_basis, transfer, send_list, near_list, near_count, far_list, coupling, group_transfer, group_coupling):
    devices = N_GRP * N_SUB
    leaf_ids = jnp.arange(LEAVES, dtype=jnp.int32)
    owner = leaf_ids // LEAF_DEV
    group_of = owner // N_SUB
    member = owner % N_SUB
    remote = near_list >= LEAF_DEV
    offset = jnp.maximum(near_list - LEAF_DEV, 0)
    sender = group_of[None, :] * N_SUB + offset // CAP
    slot_leaf = send_list[sender * N_SUB + member[None, :], offset % CAP]
    source_leaf = jnp.where(remote, sender * LEAF_DEV + slot_leaf, owner[None, :] * LEAF_DEV + near_list).astype(jnp.int32)

    def near_device(device):
        start = device * LEAF_DEV
        chosen = lax.dynamic_slice_in_dim(source_leaf, start, LEAF_DEV, 1)
        counts = lax.dynamic_slice_in_dim(near_count, start, LEAF_DEV, 0)
        targets = lax.dynamic_slice_in_dim(coords, start, LEAF_DEV, 2)

        def one_entry(entry, total):
            picked = lax.dynamic_index_in_dim(chosen, entry, 0, keepdims=False)
            values = jnp.take(sources, picked, axis=2)
            points = jnp.take(coords, picked, axis=2)
            return total + near_block(targets, points, values, entry < counts)
        return lax.fori_loop(0, NEAR, one_entry, jnp.zeros((RHS, LEAF, LEAF_DEV), jnp.float32))
    stacked = lax.map(near_device, jnp.arange(devices, dtype=jnp.int32))
    near = jnp.transpose(stacked, (1, 2, 0, 3)).reshape(RHS, LEAF, LEAVES)
    skel = jnp.einsum('ktl,rtl->krl', leaf_basis, sources, precision=HIGH)
    lifted = jnp.einsum('jkl,krl->jrl', transfer, skel, precision=HIGH)
    parent_skel = lax.optimization_barrier(jnp.sum(lifted.reshape(RANK, RHS, PARENTS, 8), axis=3))
    parent_group = jnp.arange(PARENTS, dtype=jnp.int32) // PAR_GRP
    partner = (parent_group[None, :] * PAR_GRP + far_list).astype(jnp.int32)
    partners = parent_skel[:, :, partner]
    local_field = jnp.einsum('kjfp,jrfp->krp', coupling, partners, precision=HIGH)
    parts = jnp.einsum('kjp,jrp->krp', group_transfer, parent_skel, precision=HIGH)
    group_skel = lax.optimization_barrier(jnp.sum(parts.reshape(RANK, RHS, N_GRP, PAR_GRP), axis=3))
    others = 1.0 - jnp.eye(N_GRP, dtype=jnp.float32)
    inflow = jnp.einsum('kjgh,jrh->krg', group_coupling * others[None, None, :, :], group_skel, precision=HIGH)
    field = local_field + jnp.einsum('jkp,jrp->krp', group_transfer, inflow[:, :, parent_group], precision=HIGH)
    leaf_field = jnp.einsum('jkl,jrl->krl', transfer, jnp.repeat(field, 8, axis=2), precision=HIGH)
    far = jnp.einsum('ktl,krl->rtl', leaf_basis, leaf_field, precision=HIGH)
    return near + far
```

```python
import math

import jax
import jax.numpy as jnp
from jax import lax
from jax.experimental import pallas as pl
from jax.experimental.pallas import tpu as pltpu
from jax.sharding import PartitionSpec as P

INV_FOUR_PI = 1.0 / (4.0 * math.pi)
EPS_SQ = 0.01
HIGH = lax.Precision.HIGHEST
MESH = pl.DeviceIdType.MESH
LANES = 128
CHILDREN = 8


def mm(a, b, dims=((1,), (0,))):
    return lax.dot_general(a, b, (dims, ((), ())), precision=HIGH, preferred_element_type=jnp.float32)


def lane_block(rows):
    return lax.broadcasted_iota(jnp.int32, (rows, LANES), 1) // 32


def pick_blocks(parts):
    blk = lane_block(parts[0].shape[0])
    out = parts[3]
    for a in (2, 1, 0):
        out = jnp.where(blk == a, parts[a], out)
    return out


def fold(full):
    y = pick_blocks([full[32 * a:32 * a + 32] for a in range(4)])
    y = y + pltpu.roll(y, 64, 1)
    return y + pltpu.roll(y, 32, 1)


def dense(y):
    return pick_blocks([y[8 * a:8 * a + 8] for a in range(4)])


def exchange_kernel(n_grp, n_sub, par, cap,
                    send_list, far_idx, own, own_pts, basis, trans, coup, gt_up, gt_down, gcoup,
                    recv, far,
                    send, ps_all, gs_all, field, send_sem, recv_sem, ps_send, ps_recv, gs_send, gs_recv):
    me = lax.axis_index("sub")
    grp = lax.axis_index("grp")
    barrier = pltpu.get_barrier_semaphore()
    for o in range(1, n_sub):
        pl.semaphore_signal(barrier, inc=1, device_id={"sub": lax.rem(me + o, n_sub)}, device_id_type=MESH)
    for o in range(1, n_grp):
        pl.semaphore_signal(barrier, inc=1, device_id={"grp": lax.rem(grp + o, n_grp)}, device_id_type=MESH)

    left = lax.broadcasted_iota(jnp.int32, (16, LANES), 1) < 64
    left8 = lax.broadcasted_iota(jnp.int32, (8, LANES), 1) < 64

    def pack(peer, carry):
        tops = []
        for s in range(cap):
            leaf = send_list[peer, s]
            block = own[leaf]
            send[peer, 16 * s:16 * s + 16, :] = jnp.where(left, block[:16], block[16:])
            tops.append(own_pts[leaf])
        for p in range(cap // 2):
            both = jnp.where(left8, tops[2 * p], tops[2 * p + 1])
            for d in range(3):
                row = 16 * cap + (cap // 2) * d + p
                send[peer, row:row + 1, :] = both[d:d + 1]
        return carry

    lax.fori_loop(0, n_sub, pack, 0)
    pl.semaphore_wait(barrier, n_sub - 1 + n_grp - 1)

    def value_copy(o):
        peer = lax.rem(me + o, n_sub)
        return pltpu.make_async_remote_copy(
            src_ref=send.at[peer], dst_ref=recv.at[me], send_sem=send_sem.at[o], recv_sem=recv_sem.at[o],
            device_id={"sub": peer}, device_id_type=MESH)

    for o in range(1, n_sub):
        value_copy(o).start()
    recv[me] = send[me]

    same = (lax.broadcasted_iota(jnp.int32, (256, 256), 0) // 32
            == lax.broadcasted_iota(jnp.int32, (256, 256), 1) // 32)

    def lift(c, carry):
        first = pl.multiple_of(c * CHILDREN, CHILDREN)
        rows = pl.ds(pl.multiple_of(c * 256, 256), 256)
        vals = own[pl.ds(first, CHILDREN)].reshape(256, LANES)[:, :64]
        skel = jnp.where(same, mm(basis[rows, :], vals, ((1,), (1,))), 0.0)
        up = mm(trans[rows, :], skel, ((0,), (0,)))
        y = up[:, :LANES] + up[:, LANES:]
        y = y + pltpu.roll(y, 64, 1)
        y = y + pltpu.roll(y, 32, 1)
        ps_all[me * (par + 1) + c] = dense(y)
        return carry

    lax.fori_loop(0, par, lift, 0)
    mine = ps_all[pl.ds(me * (par + 1), par)].reshape(par * 8, LANES)
    ps_all[me * (par + 1) + par] = dense(fold(mm(gt_up[...], mine)))

    def skel_copy(o):
        part = ps_all.at[pl.ds(me * (par + 1), par + 1)]
        return pltpu.make_async_remote_copy(
            src_ref=part, dst_ref=part, send_sem=ps_send.at[o], recv_sem=ps_recv.at[o],
            device_id={"sub": lax.rem(me + o, n_sub)}, device_id_type=MESH)

    for o in range(1, n_sub):
        skel_copy(o).start()
    for o in range(1, n_sub):
        skel_copy(o).wait()

    total = ps_all[par]
    for m in range(1, n_sub):
        total = total + ps_all[m * (par + 1) + par]
    gs_all[grp] = total

    def group_copy(o):
        return pltpu.make_async_remote_copy(
            src_ref=gs_all.at[grp], dst_ref=gs_all.at[grp], send_sem=gs_send.at[o], recv_sem=gs_recv.at[o],
            device_id={"grp": lax.rem(grp + o, n_grp)}, device_id_type=MESH)

    for o in range(1, n_grp):
        group_copy(o).start()

    def local(c, carry):
        partners = jnp.concatenate([ps_all[far_idx[f, c]] for f in range(16)], axis=0)
        field[c] = fold(mm(coup[c], partners))
        return carry

    lax.fori_loop(0, par, local, 0)
    for o in range(1, n_grp):
        group_copy(o).wait()
    inflow = fold(mm(gcoup[...], gs_all[...].reshape(n_grp * 8, LANES)))

    def down(c, carry):
        rows = pl.ds(pl.multiple_of(c * 256, 256), 256)
        here = field[c] + mm(gt_down[pl.ds(pl.multiple_of(c * 32, 32), 32), :], inflow)
        leaf_field = mm(here.T, trans[rows, :], ((1,), (1,)))
        spread = jnp.where(same, jnp.concatenate([leaf_field, leaf_field], axis=0), 0.0)
        far[rows, :] = mm(spread, basis[rows, :])
        return carry

    lax.fori_loop(0, par, down, 0)
    for o in range(1, n_sub):
        value_copy(o).wait()


def near_kernel(n_sub, cap, slots, leaves, idx, own, own_pts, recv, far, out, vals, pts):
    left8 = lax.broadcasted_iota(jnp.int32, (8, LANES), 1) < 64
    left16 = lax.broadcasted_iota(jnp.int32, (16, LANES), 1) < 64
    left64 = lax.broadcasted_iota(jnp.int32, (64, LANES), 1) < 64

    def put(slot, block):
        high = block.astype(jnp.bfloat16)
        vals[slot, 0:32, :] = high
        vals[slot, 32:64, :] = (block - high.astype(jnp.float32)).astype(jnp.bfloat16)

    def keep(l, carry):
        put(l, own[l])
        pts[l] = own_pts[l]
        return carry

    lax.fori_loop(0, leaves, keep, 0, unroll=8)

    def unpack(peer, carry):
        base = leaves + peer * cap
        for s in range(cap):
            d = recv[peer, 16 * s:16 * s + 16, :]
            turned = pltpu.roll(d, 64, 1)
            put(base + s, jnp.concatenate([jnp.where(left16, d, turned), jnp.where(left16, turned, d)], axis=0))
        for d in range(3):
            start = 16 * cap + (cap // 2) * d
            tile = recv[peer, start:start + cap // 2, :]
            turned = pltpu.roll(tile, 64, 1)
            even, odd = jnp.where(left8, tile, turned), jnp.where(left8, turned, tile)
            for p in range(cap // 2):
                pts[base + 2 * p, d:d + 1, :] = even[p:p + 1]
                pts[base + 2 * p + 1, d:d + 1, :] = odd[p:p + 1]
        return carry

    lax.fori_loop(0, n_sub, unpack, 0)
    vals[slots] = jnp.zeros((64, LANES), jnp.bfloat16)
    pts[slots] = jnp.zeros((8, LANES), jnp.float32)

    def one_leaf(i, carry):
        cols = own_pts[i].T
        target = [jnp.broadcast_to(cols[:64, d:d + 1], (64, LANES)) for d in range(3)]
        values, highs, lows = [], [], []
        for p in range(4):
            a, b = idx[2 * p, i], idx[2 * p + 1, i]
            points = jnp.where(left8, pts[a], pts[b])
            values.append(jnp.where(left64, vals[a], vals[b]))
            dist = EPS_SQ
            for d in range(3):
                diff = target[d] - points[d:d + 1, :]
                dist = dist + diff * diff
            kern = lax.rsqrt(dist)
            high = kern.astype(jnp.bfloat16)
            highs.append(high)
            lows.append((kern - high.astype(jnp.float32)).astype(jnp.bfloat16))
        v = jnp.concatenate(values, axis=1)
        nt = (((1,), (1,)), ((), ()))
        main = lax.dot_general(v, jnp.concatenate(highs, axis=1), nt, preferred_element_type=jnp.float32)
        rest = lax.dot_general(v[:32], jnp.concatenate(lows, axis=1), nt, preferred_element_type=jnp.float32)
        out[i] = far[i] + INV_FOUR_PI * (main[:32] + main[32:] + rest)
        return carry

    lax.fori_loop(0, leaves, one_leaf, 0, unroll=2)


def body(
    sources,
    coords,
    leaf_basis,
    transfer,
    send_list,
    near_list,
    near_count,
    far_list,
    coupling,
    group_transfer,
    group_coupling,
):
    n_sub = lax.axis_size("sub")
    n_grp = lax.axis_size("grp")
    leaves = sources.shape[2]
    par = leaves // CHILDREN
    cap = send_list.shape[1]
    slots = leaves + n_sub * cap
    near_entries = near_list.shape[0]
    f32 = jnp.float32

    x = jnp.transpose(sources, (2, 0, 1))
    own = jnp.concatenate([x, x], axis=2)
    y = jnp.transpose(coords, (2, 0, 1))
    own_pts = jnp.pad(jnp.concatenate([y, y], axis=2), ((0, 0), (0, 5), (0, 0)))
    basis = jnp.transpose(leaf_basis, (2, 0, 1)).reshape(leaves * 32, 64)
    trans = jnp.transpose(transfer, (2, 1, 0)).reshape(leaves * 32, 32)
    coup = coupling.reshape(32, 4, 8, 16, par).transpose(4, 1, 0, 3, 2).reshape(par, 128, 128)
    gt_up = group_transfer.reshape(32, 4, 8, par).transpose(1, 0, 3, 2).reshape(128, par * 8)
    gt_down = jnp.transpose(group_transfer, (2, 1, 0)).reshape(par * 32, 32)
    my_group = lax.axis_index("grp")
    row = lax.dynamic_index_in_dim(group_coupling, my_group, 2, keepdims=False)
    others = (jnp.arange(n_grp, dtype=jnp.int32) != my_group).astype(f32)
    gcoup = (row * others).reshape(32, 4, 8, n_grp).transpose(1, 0, 3, 2).reshape(128, n_grp * 8)
    far_idx = far_list + far_list // par
    live = jnp.arange(near_entries, dtype=jnp.int32)[:, None] < near_count[None, :]
    idx = jnp.pad(jnp.where(live, near_list, slots), ((0, 8 - near_entries), (0, 0)), constant_values=slots)

    vmem = pl.BlockSpec(memory_space=pltpu.VMEM)
    smem = pl.BlockSpec(memory_space=pltpu.SMEM)
    rows = 16 * cap + 3 * (cap // 2)
    dma = pltpu.SemaphoreType.DMA
    recv, far = pl.pallas_call(
        lambda *refs: exchange_kernel(n_grp, n_sub, par, cap, *refs),
        out_shape=(jax.ShapeDtypeStruct((n_sub, rows, LANES), f32),
                   jax.ShapeDtypeStruct((leaves * 32, 64), f32)),
        in_specs=[smem, smem] + [vmem] * 8,
        out_specs=(vmem, vmem),
        scratch_shapes=[
            pltpu.VMEM((n_sub, rows, LANES), f32),
            pltpu.VMEM((n_sub * (par + 1), 8, LANES), f32),
            pltpu.VMEM((n_grp, 8, LANES), f32),
            pltpu.VMEM((par, 32, LANES), f32),
            dma((n_sub,)), dma((n_sub,)), dma((n_sub,)), dma((n_sub,)), dma((n_grp,)), dma((n_grp,)),
        ],
        compiler_params=pltpu.CompilerParams(
            collective_id=0, has_side_effects=True, vmem_limit_bytes=48 * 2**20),
        name="exchange_far",
    )(send_list, far_idx, own, own_pts, basis, trans, coup, gt_up, gt_down, gcoup)

    out = pl.pallas_call(
        lambda *refs: near_kernel(n_sub, cap, slots, leaves, *refs),
        out_shape=jax.ShapeDtypeStruct((leaves, 32, 64), f32),
        in_specs=[smem] + [vmem] * 4,
        out_specs=vmem,
        scratch_shapes=[
            pltpu.VMEM((slots + 1, 64, LANES), jnp.bfloat16),
            pltpu.VMEM((slots + 1, 8, LANES), f32),
        ],
        compiler_params=pltpu.CompilerParams(vmem_limit_bytes=48 * 2**20),
        name="near_field",
    )(idx, own, own_pts, recv, far.reshape(leaves, 32, 64))
    return jnp.transpose(out, (1, 2, 0))


def solution(mesh):
    whole = ("grp", "sub")
    return jax.shard_map(
        body,
        mesh=mesh,
        in_specs=(
            P(None, None, whole),
            P(None, None, whole),
            P(None, None, whole),
            P(None, None, whole),
            P(whole, None),
            P(None, whole),
            P(whole),
            P(None, whole),
            P(None, None, None, whole),
            P(None, None, whole),
            P(),
        ),
        out_specs=P(None, None, whole),
        check_vma=False,
    )
```

```python
import math

import jax
import jax.numpy as jnp
from jax import lax
from jax.experimental import pallas as pl
from jax.experimental.pallas import tpu as pltpu
from jax.sharding import PartitionSpec as P

INV_FOUR_PI = 1.0 / (4.0 * math.pi)
EPS_SQ = 0.01
MESH = pl.DeviceIdType.MESH
LANES = 128
CHILDREN = 8


def halves(x):
    high = x.astype(jnp.bfloat16)
    return high, (x - high.astype(jnp.float32)).astype(jnp.bfloat16)


def mm(a, b, dims=((1,), (0,))):
    def dot(x, y):
        return lax.dot_general(x, y, (dims, ((), ())), preferred_element_type=jnp.float32)
    a0, a1 = halves(a)
    b0, b1 = halves(b)
    return dot(a0, b0) + (dot(a0, b1) + dot(a1, b0))


def lane_block(rows):
    return lax.broadcasted_iota(jnp.int32, (rows, LANES), 1) // 32


def pick_blocks(parts):
    blk = lane_block(parts[0].shape[0])
    out = parts[3]
    for a in (2, 1, 0):
        out = jnp.where(blk == a, parts[a], out)
    return out


def spread_lanes(y):
    y = jnp.where(lane_block(y.shape[0]) == 0, y, 0.0)
    y = y + pltpu.roll(y, 32, 1)
    return y + pltpu.roll(y, 64, 1)


def loose(block):
    return jnp.concatenate([block] + [pltpu.roll(block, LANES - 32 * a, 1) for a in range(1, 4)], axis=0)


def dense(y):
    return pick_blocks([y[8 * a:8 * a + 8] for a in range(4)])


def exchange_kernel(n_grp, n_sub, par, cap,
                    send_list, far_list, own, own_pts, basis, trans, gt, gcoup, coup_hbm,
                    recv, far,
                    send, ps_all, gs_all, loose_all, field, coup, send_sem, recv_sem, ps_send, ps_recv, gs_send,
                    gs_recv, coup_sem):
    me = lax.axis_index("sub")
    grp = lax.axis_index("grp")
    barrier = pltpu.get_barrier_semaphore()
    for o in range(1, n_sub):
        pl.semaphore_signal(barrier, inc=1, device_id={"sub": lax.rem(me + o, n_sub)}, device_id_type=MESH)
    for o in range(1, n_grp):
        pl.semaphore_signal(barrier, inc=1, device_id={"grp": lax.rem(grp + o, n_grp)}, device_id_type=MESH)

    coup_copy = pltpu.make_async_copy(coup_hbm, coup, coup_sem)
    coup_copy.start()
    same = (lax.broadcasted_iota(jnp.int32, (256, 256), 0) // 32
            == lax.broadcasted_iota(jnp.int32, (256, 256), 1) // 32)

    def lift(c, carry):
        first = pl.multiple_of(c * CHILDREN, CHILDREN)
        rows = pl.ds(pl.multiple_of(c * 256, 256), 256)
        vals = own[pl.ds(first, CHILDREN)].reshape(256, LANES)[:, :64]
        skel = jnp.where(same, mm(basis[rows, :], vals, ((1,), (1,))), 0.0)
        up = mm(trans[rows, :], skel, ((0,), (0,)))
        y = up[:, :LANES] + up[:, LANES:]
        y = y + pltpu.roll(y, 64, 1)
        y = y + pltpu.roll(y, 32, 1)
        ps_all[me * (par + 1) + c] = dense(y)
        return carry + mm(gt[pl.ds(c, 32, stride=par), :], y)

    part = lax.fori_loop(0, par, lift, jnp.zeros((32, LANES), jnp.float32))
    ps_all[me * (par + 1) + par] = dense(part)
    pl.semaphore_wait(barrier, n_sub - 1 + n_grp - 1)

    def skel_copy(o):
        part = ps_all.at[pl.ds(me * (par + 1), par + 1)]
        return pltpu.make_async_remote_copy(
            src_ref=part, dst_ref=part, send_sem=ps_send.at[o], recv_sem=ps_recv.at[o],
            device_id={"sub": lax.rem(me + o, n_sub)}, device_id_type=MESH)

    for o in range(1, n_sub):
        skel_copy(o).start()

    left = lax.broadcasted_iota(jnp.int32, (16, LANES), 1) < 64
    left8 = lax.broadcasted_iota(jnp.int32, (8, LANES), 1) < 64

    def pack(peer, carry):
        tops = []
        for s in range(cap):
            leaf = send_list[peer, s]
            block = own[leaf]
            send[peer, 16 * s:16 * s + 16, :] = jnp.where(left, block[:16], block[16:])
            tops.append(own_pts[leaf])
        for p in range(cap // 2):
            both = jnp.where(left8, tops[2 * p], tops[2 * p + 1])
            for d in range(3):
                row = 16 * cap + (cap // 2) * d + p
                send[peer, row:row + 1, :] = both[d:d + 1]
        return carry

    lax.fori_loop(0, n_sub, pack, 0)
    def value_copy(o):
        peer = lax.rem(me + o, n_sub)
        return pltpu.make_async_remote_copy(
            src_ref=send.at[peer], dst_ref=recv.at[me], send_sem=send_sem.at[o], recv_sem=recv_sem.at[o],
            device_id={"sub": peer}, device_id_type=MESH)

    for o in range(1, n_sub):
        value_copy(o).start()
    recv[me] = send[me]

    for o in range(1, n_sub):
        skel_copy(o).wait()

    total = ps_all[par]
    for m in range(1, n_sub):
        total = total + ps_all[m * (par + 1) + par]
    gs_all[grp] = total

    def group_copy(o):
        return pltpu.make_async_remote_copy(
            src_ref=gs_all.at[grp], dst_ref=gs_all.at[grp], send_sem=gs_send.at[o], recv_sem=gs_recv.at[o],
            device_id={"grp": lax.rem(grp + o, n_grp)}, device_id_type=MESH)

    for o in range(1, n_grp):
        group_copy(o).start()

    def loosen(m, carry):
        for c in range(par):
            loose_all[m * par + c] = loose(ps_all[m * (par + 1) + c])
        return carry

    lax.fori_loop(0, n_sub, loosen, 0)
    coup_copy.wait()

    def local(c, carry):
        partners = jnp.concatenate([loose_all[far_list[f, c]] for f in range(16)], axis=0)
        blocks = jnp.concatenate([coup[pl.ds(f * par + c, 32, stride=16 * par), :] for f in range(16)], axis=1)
        field[c] = spread_lanes(mm(blocks, partners))
        return carry

    lax.fori_loop(0, par, local, 0)
    for o in range(1, n_grp):
        group_copy(o).wait()
    inflow = jnp.zeros((32, LANES), jnp.float32)
    for h in range(n_grp):
        live = jnp.where(grp == h, 0.0, 1.0)
        block = gcoup[pl.ds(grp * n_grp + h, 32, stride=n_grp * n_grp), :]
        inflow = inflow + mm(block * live, loose(gs_all[h]))
    inflow = spread_lanes(inflow)

    def down(c, carry):
        rows = pl.ds(pl.multiple_of(c * 256, 256), 256)
        here = field[c] + mm(gt[pl.ds(c, 32, stride=par), :], inflow, ((0,), (0,)))
        leaf_field = mm(here.T, trans[rows, :], ((1,), (1,)))
        spread = jnp.where(same, jnp.concatenate([leaf_field, leaf_field], axis=0), 0.0)
        far[rows, :] = mm(spread, basis[rows, :])
        return carry

    lax.fori_loop(0, par, down, 0)
    for o in range(1, n_sub):
        value_copy(o).wait()


def near_kernel(n_sub, cap, slots, leaves, idx, own, own_pts, recv, far, out, vals, pts):
    left8 = lax.broadcasted_iota(jnp.int32, (8, LANES), 1) < 64
    left16 = lax.broadcasted_iota(jnp.int32, (16, LANES), 1) < 64

    def put(slot, block):
        high = block.astype(jnp.bfloat16).astype(jnp.float32)
        both = jnp.concatenate([high, block - high], axis=0)
        vals[slot] = both.T[:64].astype(jnp.bfloat16)

    def keep(l, carry):
        put(l, own[l])
        pts[l] = own_pts[l]
        return carry

    lax.fori_loop(0, leaves, keep, 0, unroll=8)

    def unpack(peer, carry):
        base = leaves + peer * cap
        for s in range(cap):
            d = recv[peer, 16 * s:16 * s + 16, :]
            turned = pltpu.roll(d, 64, 1)
            put(base + s, jnp.concatenate([jnp.where(left16, d, turned), jnp.where(left16, turned, d)], axis=0))
        for d in range(3):
            start = 16 * cap + (cap // 2) * d
            tile = recv[peer, start:start + cap // 2, :]
            turned = pltpu.roll(tile, 64, 1)
            even, odd = jnp.where(left8, tile, turned), jnp.where(left8, turned, tile)
            for p in range(cap // 2):
                pts[base + 2 * p, d:d + 1, :] = even[p:p + 1]
                pts[base + 2 * p + 1, d:d + 1, :] = odd[p:p + 1]
        return carry

    lax.fori_loop(0, n_sub, unpack, 0)
    vals[slots] = jnp.zeros((64, 64), jnp.bfloat16)
    pts[slots] = jnp.zeros((8, LANES), jnp.float32)

    def one_leaf(i, carry):
        cols = own_pts[i].T
        target = [jnp.broadcast_to(cols[:64, d:d + 1], (64, LANES)) for d in range(3)]
        values, highs, lows = [], [], []
        for p in range(4):
            a, b = idx[2 * p, i], idx[2 * p + 1, i]
            points = jnp.where(left8, pts[a], pts[b])
            values += [vals[a], vals[b]]
            dist = EPS_SQ
            for d in range(3):
                diff = target[d] - points[d:d + 1, :]
                dist = dist + diff * diff
            kern = lax.rsqrt(dist)
            high = kern.astype(jnp.bfloat16)
            highs.append(high)
            lows.append((kern - high.astype(jnp.float32)).astype(jnp.bfloat16))
        kernels = jnp.concatenate([jnp.concatenate(highs, axis=1), jnp.concatenate(lows, axis=1)], axis=0)
        full = jnp.dot(kernels, jnp.concatenate(values, axis=0), preferred_element_type=jnp.float32)
        top = full[:64]
        near = top[:, :32] + top[:, 32:] + full[64:, :32]
        out[i] = far[i] + INV_FOUR_PI * near.T
        return carry

    lax.fori_loop(0, leaves, one_leaf, 0, unroll=4)


def body(
    sources,
    coords,
    leaf_basis,
    transfer,
    send_list,
    near_list,
    near_count,
    far_list,
    coupling,
    group_transfer,
    group_coupling,
):
    n_sub = lax.axis_size("sub")
    n_grp = lax.axis_size("grp")
    leaves = sources.shape[2]
    par = leaves // CHILDREN
    cap = send_list.shape[1]
    slots = leaves + n_sub * cap
    near_entries = near_list.shape[0]
    f32 = jnp.float32

    x = jnp.transpose(sources, (2, 0, 1))
    own = jnp.concatenate([x, x], axis=2)
    y = jnp.transpose(coords, (2, 0, 1))
    own_pts = jnp.pad(jnp.concatenate([y, y], axis=2), ((0, 0), (0, 5), (0, 0)))
    basis = jnp.transpose(leaf_basis, (2, 0, 1)).reshape(leaves * 32, 64)
    trans = jnp.transpose(transfer, (2, 1, 0)).reshape(leaves * 32, 32)
    coup = jnp.transpose(coupling, (0, 2, 3, 1)).reshape(32 * 16 * par, 32)
    gt = jnp.transpose(group_transfer, (0, 2, 1)).reshape(32 * par, 32)
    gcoup = jnp.transpose(group_coupling, (0, 2, 3, 1)).reshape(32 * n_grp * n_grp, 32)
    live = jnp.arange(near_entries, dtype=jnp.int32)[:, None] < near_count[None, :]
    idx = jnp.pad(jnp.where(live, near_list, slots), ((0, 8 - near_entries), (0, 0)), constant_values=slots)

    vmem = pl.BlockSpec(memory_space=pltpu.VMEM)
    smem = pl.BlockSpec(memory_space=pltpu.SMEM)
    rows = 16 * cap + 3 * (cap // 2)
    dma = pltpu.SemaphoreType.DMA
    recv, far = pl.pallas_call(
        lambda *refs: exchange_kernel(n_grp, n_sub, par, cap, *refs),
        out_shape=(jax.ShapeDtypeStruct((n_sub, rows, LANES), f32),
                   jax.ShapeDtypeStruct((leaves * 32, 64), f32)),
        in_specs=[smem, smem] + [vmem] * 6 + [pl.BlockSpec(memory_space=pl.ANY)],
        out_specs=(vmem, vmem),
        scratch_shapes=[
            pltpu.VMEM((n_sub, rows, LANES), f32),
            pltpu.VMEM((n_sub * (par + 1), 8, LANES), f32),
            pltpu.VMEM((n_grp, 8, LANES), f32),
            pltpu.VMEM((n_sub * par, 32, LANES), f32),
            pltpu.VMEM((par, 32, LANES), f32),
            pltpu.VMEM((32 * 16 * par, 32), f32),
            dma((n_sub,)), dma((n_sub,)), dma((n_sub,)), dma((n_sub,)), dma((n_grp,)), dma((n_grp,)), dma,
        ],
        compiler_params=pltpu.CompilerParams(
            collective_id=0, has_side_effects=True, vmem_limit_bytes=48 * 2**20),
        name="exchange_far",
    )(send_list, far_list, own, own_pts, basis, trans, gt, gcoup, coup)

    out = pl.pallas_call(
        lambda *refs: near_kernel(n_sub, cap, slots, leaves, *refs),
        out_shape=jax.ShapeDtypeStruct((leaves, 32, 64), f32),
        in_specs=[smem] + [vmem] * 4,
        out_specs=vmem,
        scratch_shapes=[
            pltpu.VMEM((slots + 1, 64, 64), jnp.bfloat16),
            pltpu.VMEM((slots + 1, 8, LANES), f32),
        ],
        compiler_params=pltpu.CompilerParams(vmem_limit_bytes=48 * 2**20),
        name="near_field",
    )(idx, own, own_pts, recv, far.reshape(leaves, 32, 64))
    return jnp.transpose(out, (1, 2, 0))


def solution(mesh):
    whole = ("grp", "sub")
    return jax.shard_map(
        body,
        mesh=mesh,
        in_specs=(
            P(None, None, whole),
            P(None, None, whole),
            P(None, None, whole),
            P(None, None, whole),
            P(whole, None),
            P(None, whole),
            P(whole),
            P(None, whole),
            P(None, None, None, whole),
            P(None, None, whole),
            P(),
        ),
        out_specs=P(None, None, whole),
        check_vma=False,
    )
```

```python
import math

import jax
import jax.numpy as jnp
from jax import lax
from jax.experimental import pallas as pl
from jax.experimental.pallas import tpu as pltpu
from jax.sharding import PartitionSpec as P

INV_FOUR_PI = 1.0 / (4.0 * math.pi)
EPS_SQ = 0.01
MESH = pl.DeviceIdType.MESH
LANES = 128
CHILDREN = 8


def halves(x):
    high = x.astype(jnp.bfloat16)
    return high, (x - high.astype(jnp.float32)).astype(jnp.bfloat16)


def mm(a, b, dims=((1,), (0,))):
    def dot(x, y):
        return lax.dot_general(x, y, (dims, ((), ())), preferred_element_type=jnp.float32)
    a0, a1 = halves(a)
    b0, b1 = halves(b)
    return dot(a0, b0) + (dot(a0, b1) + dot(a1, b0))


def lane_block(rows):
    return lax.broadcasted_iota(jnp.int32, (rows, LANES), 1) // 32


def pick_blocks(parts):
    blk = lane_block(parts[0].shape[0])
    out = parts[3]
    for a in (2, 1, 0):
        out = jnp.where(blk == a, parts[a], out)
    return out


def spread_lanes(y):
    y = jnp.where(lane_block(y.shape[0]) == 0, y, 0.0)
    y = y + pltpu.roll(y, 32, 1)
    return y + pltpu.roll(y, 64, 1)


def loose(block):
    return jnp.concatenate([block] + [pltpu.roll(block, LANES - 32 * a, 1) for a in range(1, 4)], axis=0)


def dense(y):
    return pick_blocks([y[8 * a:8 * a + 8] for a in range(4)])


def exchange_kernel(n_grp, n_sub, par, cap,
                    send_list, far_list, own, own_pts, basis, trans, gt, gcoup, coup_hbm,
                    recv, far,
                    send, ps_all, gs_all, loose_all, field, coup, send_sem, recv_sem, ps_send, ps_recv, gs_send,
                    gs_recv, coup_sem):
    me = lax.axis_index("sub")
    grp = lax.axis_index("grp")
    barrier = pltpu.get_barrier_semaphore()
    for o in range(1, n_sub):
        pl.semaphore_signal(barrier, inc=1, device_id={"sub": lax.rem(me + o, n_sub)}, device_id_type=MESH)
    for o in range(1, n_grp):
        pl.semaphore_signal(barrier, inc=1, device_id={"grp": lax.rem(grp + o, n_grp)}, device_id_type=MESH)

    coup_copy = pltpu.make_async_copy(coup_hbm, coup, coup_sem)
    coup_copy.start()
    same = (lax.broadcasted_iota(jnp.int32, (256, 256), 0) // 32
            == lax.broadcasted_iota(jnp.int32, (256, 256), 1) // 32)

    def lift(c, carry):
        first = pl.multiple_of(c * CHILDREN, CHILDREN)
        rows = pl.ds(pl.multiple_of(c * 256, 256), 256)
        vals = jnp.concatenate([own[first + i] for i in range(CHILDREN)], axis=1)
        skel = jnp.where(same, mm(basis[rows, :], vals), 0.0)
        up = mm(trans[rows, :], skel, ((0,), (0,)))
        y = up[:, :LANES] + up[:, LANES:]
        y = y + pltpu.roll(y, 64, 1)
        y = y + pltpu.roll(y, 32, 1)
        ps_all[me * (par + 1) + c] = dense(y)
        return carry + mm(gt[pl.ds(c, 32, stride=par), :], y)

    part = lax.fori_loop(0, par, lift, jnp.zeros((32, LANES), jnp.float32))
    ps_all[me * (par + 1) + par] = dense(part)
    pl.semaphore_wait(barrier, n_sub - 1 + n_grp - 1)

    def skel_copy(o):
        part = ps_all.at[pl.ds(me * (par + 1), par + 1)]
        return pltpu.make_async_remote_copy(
            src_ref=part, dst_ref=part, send_sem=ps_send.at[o], recv_sem=ps_recv.at[o],
            device_id={"sub": lax.rem(me + o, n_sub)}, device_id_type=MESH)

    for o in range(1, n_sub):
        skel_copy(o).start()

    left8 = lax.broadcasted_iota(jnp.int32, (8, LANES), 1) < 64

    def pack(peer, carry):
        tops = []
        for s in range(cap):
            leaf = send_list[peer, s]
            block = own[leaf]
            send[peer, 16 * s:16 * s + 16, :] = jnp.concatenate([block[16 * a:16 * a + 16] for a in range(4)], axis=1)
            tops.append(own_pts[leaf])
        for p in range(cap // 2):
            both = jnp.where(left8, tops[2 * p], tops[2 * p + 1])
            for d in range(3):
                row = 16 * cap + (cap // 2) * d + p
                send[peer, row:row + 1, :] = both[d:d + 1]
        return carry

    lax.fori_loop(0, n_sub, pack, 0)
    def value_copy(o):
        peer = lax.rem(me + o, n_sub)
        return pltpu.make_async_remote_copy(
            src_ref=send.at[peer], dst_ref=recv.at[me], send_sem=send_sem.at[o], recv_sem=recv_sem.at[o],
            device_id={"sub": peer}, device_id_type=MESH)

    for o in range(1, n_sub):
        value_copy(o).start()
    recv[me] = send[me]

    for o in range(1, n_sub):
        skel_copy(o).wait()

    total = ps_all[par]
    for m in range(1, n_sub):
        total = total + ps_all[m * (par + 1) + par]
    gs_all[grp] = total

    def group_copy(o):
        return pltpu.make_async_remote_copy(
            src_ref=gs_all.at[grp], dst_ref=gs_all.at[grp], send_sem=gs_send.at[o], recv_sem=gs_recv.at[o],
            device_id={"grp": lax.rem(grp + o, n_grp)}, device_id_type=MESH)

    for o in range(1, n_grp):
        group_copy(o).start()

    def loosen(m, carry):
        for c in range(par):
            loose_all[m * par + c] = loose(ps_all[m * (par + 1) + c])
        return carry

    lax.fori_loop(0, n_sub, loosen, 0)
    coup_copy.wait()

    def local(c, carry):
        partners = jnp.concatenate([loose_all[far_list[f, c]] for f in range(16)], axis=0)
        blocks = jnp.concatenate([coup[pl.ds(f * par + c, 32, stride=16 * par), :] for f in range(16)], axis=1)
        field[c] = spread_lanes(mm(blocks, partners))
        return carry

    lax.fori_loop(0, par, local, 0)
    for o in range(1, n_grp):
        group_copy(o).wait()
    inflow = jnp.zeros((32, LANES), jnp.float32)
    for h in range(n_grp):
        live = jnp.where(grp == h, 0.0, 1.0)
        block = gcoup[pl.ds(grp * n_grp + h, 32, stride=n_grp * n_grp), :]
        inflow = inflow + mm(block * live, loose(gs_all[h]))
    inflow = spread_lanes(inflow)

    def down(c, carry):
        rows = pl.ds(pl.multiple_of(c * 256, 256), 256)
        here = field[c] + mm(gt[pl.ds(c, 32, stride=par), :], inflow, ((0,), (0,)))
        leaf_field = mm(here.T, trans[rows, :], ((1,), (1,)))
        spread = jnp.where(same, jnp.concatenate([leaf_field, leaf_field], axis=0), 0.0)
        far[rows, :] = mm(spread, basis[rows, :])
        return carry

    lax.fori_loop(0, par, down, 0)
    for o in range(1, n_sub):
        value_copy(o).wait()


def thirds(x):
    terms = []
    for _ in range(3):
        term = x.astype(jnp.bfloat16).astype(jnp.float32)
        terms.append(term)
        x = x - term
    return terms


def near_kernel(n_sub, cap, slots, leaves, idx, own, own_pts, recv, far, out, vals, source, target):
    left8 = lax.broadcasted_iota(jnp.int32, (8, LANES), 1) < 64
    left48 = lax.broadcasted_iota(jnp.int32, (48, LANES), 1) < 64
    first16 = lax.broadcasted_iota(jnp.int32, (16, LANES), 1) < 32
    first64 = lax.broadcasted_iota(jnp.int32, (64, 64), 1) < 32
    row = lax.broadcasted_iota(jnp.int32, (8, LANES), 0)

    def point_rows(tile):
        centred = jnp.where(row < 3, tile - 1.0, 0.0)
        return centred, jnp.sum(centred * centred, axis=0, keepdims=True)

    def put_source(slot, tile):
        y, norm = point_rows(tile)
        u = thirds(jnp.where(row < 3, y, jnp.where(row == 3, norm, jnp.where(row == 4, 1.0, 0.0))))
        rows = jnp.concatenate([u[0], u[1], u[0], u[1], u[2], u[0]], axis=0)
        source[slot] = rows.astype(jnp.bfloat16)

    def put_target(slot, tile):
        x, norm = point_rows(tile)
        w = thirds(jnp.where(row < 3, -2.0 * x, jnp.where(row == 3, 1.0, jnp.where(row == 4, norm + EPS_SQ, 0.0))))
        rows = jnp.concatenate([w[0], w[0], w[1], w[1], w[0], w[2]], axis=0)
        target[slot] = rows.T[:64].astype(jnp.bfloat16)

    def keep(l, carry):
        block = own[l]
        high = block.astype(jnp.bfloat16).astype(jnp.float32)
        vals[l] = jnp.concatenate([high, block - high], axis=1).astype(jnp.bfloat16)
        tile = own_pts[l]
        put_source(l, tile)
        put_target(l, tile)
        return carry

    lax.fori_loop(0, leaves, keep, 0, unroll=4)

    def unpack(peer, carry):
        base = leaves + peer * cap
        for s in range(cap):
            d = recv[peer, 16 * s:16 * s + 16, :]
            high = d.astype(jnp.bfloat16).astype(jnp.float32)
            low = d - high
            rows = []
            for a in range(4):
                h = pltpu.roll(high, LANES - 32 * a, 1) if a else high
                l = pltpu.roll(low, (LANES + 32 - 32 * a) % LANES, 1) if a != 1 else low
                rows.append(jnp.where(first16, h, l))
            vals[base + s] = jnp.concatenate(rows, axis=0)[:, :64].astype(jnp.bfloat16)
        tiles = []
        for d in range(3):
            start = 16 * cap + (cap // 2) * d
            tile = recv[peer, start:start + cap // 2, :]
            turned = pltpu.roll(tile, 64, 1)
            tiles.append((jnp.where(left8, tile, turned), jnp.where(left8, turned, tile)))
        for s in range(cap):
            parts = [jnp.broadcast_to(t[s % 2][s // 2:s // 2 + 1], (8, LANES)) for t in tiles]
            put_source(base + s, jnp.where(row == 0, parts[0], jnp.where(row == 1, parts[1], parts[2])))
        return carry

    lax.fori_loop(0, n_sub, unpack, 0)
    vals[slots] = jnp.zeros((64, 64), jnp.bfloat16)
    put_source(slots, jnp.zeros((8, LANES), jnp.float32))

    def one_leaf(i, carry):
        entries = [idx[e, i] for e in range(8)]
        points = [jnp.where(left48, source[entries[2 * p]], source[entries[2 * p + 1]]) for p in range(4)]
        dist = jnp.dot(target[i], jnp.concatenate(points, axis=1), preferred_element_type=jnp.float32)
        kern = lax.rsqrt(dist)
        high = kern.astype(jnp.bfloat16)
        low = (kern - high.astype(jnp.float32)).astype(jnp.bfloat16)
        values = jnp.concatenate([vals[e] for e in entries], axis=0)
        full = jnp.dot(jnp.concatenate([high, low], axis=0), values, preferred_element_type=jnp.float32)
        near = (full[:64] + jnp.where(first64, full[64:], 0.0)).T
        out[i] = far[i] + INV_FOUR_PI * (near[:32] + near[32:])
        return carry

    lax.fori_loop(0, leaves, one_leaf, 0, unroll=4)


def body(
    sources,
    coords,
    leaf_basis,
    transfer,
    send_list,
    near_list,
    near_count,
    far_list,
    coupling,
    group_transfer,
    group_coupling,
):
    n_sub = lax.axis_size("sub")
    n_grp = lax.axis_size("grp")
    leaves = sources.shape[2]
    par = leaves // CHILDREN
    cap = send_list.shape[1]
    slots = leaves + n_sub * cap
    near_entries = near_list.shape[0]
    f32 = jnp.float32

    own = jnp.transpose(sources, (2, 1, 0))
    y = jnp.transpose(coords, (2, 0, 1))
    own_pts = jnp.pad(jnp.concatenate([y, y], axis=2), ((0, 0), (0, 5), (0, 0)))
    basis = jnp.transpose(leaf_basis, (2, 0, 1)).reshape(leaves * 32, 64)
    trans = jnp.transpose(transfer, (2, 1, 0)).reshape(leaves * 32, 32)
    coup = jnp.transpose(coupling, (0, 2, 3, 1)).reshape(32 * 16 * par, 32)
    gt = jnp.transpose(group_transfer, (0, 2, 1)).reshape(32 * par, 32)
    gcoup = jnp.transpose(group_coupling, (0, 2, 3, 1)).reshape(32 * n_grp * n_grp, 32)
    live = jnp.arange(near_entries, dtype=jnp.int32)[:, None] < near_count[None, :]
    idx = jnp.pad(jnp.where(live, near_list, slots), ((0, 8 - near_entries), (0, 0)), constant_values=slots)

    vmem = pl.BlockSpec(memory_space=pltpu.VMEM)
    smem = pl.BlockSpec(memory_space=pltpu.SMEM)
    rows = 16 * cap + 3 * (cap // 2)
    dma = pltpu.SemaphoreType.DMA
    recv, far = pl.pallas_call(
        lambda *refs: exchange_kernel(n_grp, n_sub, par, cap, *refs),
        out_shape=(jax.ShapeDtypeStruct((n_sub, rows, LANES), f32),
                   jax.ShapeDtypeStruct((leaves * 32, 64), f32)),
        in_specs=[smem, smem] + [vmem] * 6 + [pl.BlockSpec(memory_space=pl.ANY)],
        out_specs=(vmem, vmem),
        scratch_shapes=[
            pltpu.VMEM((n_sub, rows, LANES), f32),
            pltpu.VMEM((n_sub * (par + 1), 8, LANES), f32),
            pltpu.VMEM((n_grp, 8, LANES), f32),
            pltpu.VMEM((n_sub * par, 32, LANES), f32),
            pltpu.VMEM((par, 32, LANES), f32),
            pltpu.VMEM((32 * 16 * par, 32), f32),
            dma((n_sub,)), dma((n_sub,)), dma((n_sub,)), dma((n_sub,)), dma((n_grp,)), dma((n_grp,)), dma,
        ],
        compiler_params=pltpu.CompilerParams(
            collective_id=0, has_side_effects=True, vmem_limit_bytes=48 * 2**20),
        name="exchange_far",
    )(send_list, far_list, own, own_pts, basis, trans, gt, gcoup, coup)

    out = pl.pallas_call(
        lambda *refs: near_kernel(n_sub, cap, slots, leaves, *refs),
        out_shape=jax.ShapeDtypeStruct((leaves, 32, 64), f32),
        in_specs=[smem] + [vmem] * 4,
        out_specs=vmem,
        scratch_shapes=[
            pltpu.VMEM((slots + 1, 64, 64), jnp.bfloat16),
            pltpu.VMEM((slots + 1, 48, LANES), jnp.bfloat16),
            pltpu.VMEM((leaves, 64, 48), jnp.bfloat16),
        ],
        compiler_params=pltpu.CompilerParams(vmem_limit_bytes=48 * 2**20),
        name="near_field",
    )(idx, own, own_pts, recv, far.reshape(leaves, 32, 64))
    return jnp.transpose(out, (1, 2, 0))


def solution(mesh):
    whole = ("grp", "sub")
    return jax.shard_map(
        body,
        mesh=mesh,
        in_specs=(
            P(None, None, whole),
            P(None, None, whole),
            P(None, None, whole),
            P(None, None, whole),
            P(whole, None),
            P(None, whole),
            P(whole),
            P(None, whole),
            P(None, None, None, whole),
            P(None, None, whole),
            P(),
        ),
        out_specs=P(None, None, whole),
        check_vma=False,
    )
```

```python
import math

import jax
import jax.numpy as jnp
from jax import lax
from jax.experimental import pallas as pl
from jax.experimental.pallas import tpu as pltpu
from jax.sharding import PartitionSpec as P

INV_FOUR_PI = 1.0 / (4.0 * math.pi)
EPS_SQ = 0.01
MESH = pl.DeviceIdType.MESH
LANES = 128
CHILDREN = 8
TOGETHER = 4


def halves(x):
    high = x.astype(jnp.bfloat16)
    return high, (x - high.astype(jnp.float32)).astype(jnp.bfloat16)


def mm(a, b, dims=((1,), (0,))):
    def dot(x, y):
        return lax.dot_general(x, y, (dims, ((), ())), preferred_element_type=jnp.float32)
    a0, a1 = halves(a)
    b0, b1 = halves(b)
    return dot(a0, b0) + (dot(a0, b1) + dot(a1, b0))


def lane_block(rows):
    return lax.broadcasted_iota(jnp.int32, (rows, LANES), 1) // 32


def pick_blocks(parts):
    blk = lane_block(parts[0].shape[0])
    out = parts[3]
    for a in (2, 1, 0):
        out = jnp.where(blk == a, parts[a], out)
    return out


def spread_lanes(y):
    y = jnp.where(lane_block(y.shape[0]) == 0, y, 0.0)
    y = y + pltpu.roll(y, 32, 1)
    return y + pltpu.roll(y, 64, 1)


def loose(block):
    return jnp.concatenate([block] + [pltpu.roll(block, LANES - 32 * a, 1) for a in range(1, 4)], axis=0)


def dense(y):
    return pick_blocks([y[8 * a:8 * a + 8] for a in range(4)])


def thirds(x):
    terms = []
    for _ in range(3):
        term = x.astype(jnp.bfloat16).astype(jnp.float32)
        terms.append(term)
        x = x - term
    return terms


def point_rows(tile):
    row = lax.broadcasted_iota(jnp.int32, (8, LANES), 0)
    centred = jnp.where(row < 3, tile - 1.0, 0.0)
    return row, centred, jnp.sum(centred * centred, axis=0, keepdims=True)


def source_rows(tile):
    row, y, norm = point_rows(tile)
    u = thirds(jnp.where(row < 3, y, jnp.where(row == 3, norm, jnp.where(row == 4, 1.0, 0.0))))
    return jnp.concatenate([u[0], u[1], u[0], u[1], u[2], u[0]], axis=0).astype(jnp.bfloat16)


def target_columns(tile):
    row, x, norm = point_rows(tile)
    w = thirds(jnp.where(row < 3, -2.0 * x, jnp.where(row == 3, 1.0, jnp.where(row == 4, norm + EPS_SQ, 0.0))))
    rows = jnp.concatenate([w[0], w[0], w[1], w[1], w[0], w[2]], axis=0)
    return rows.T[:64].astype(jnp.bfloat16)


def unpack(cap, base, got, vals, source):
    first16 = lax.broadcasted_iota(jnp.int32, (16, LANES), 1) < 32
    left8 = lax.broadcasted_iota(jnp.int32, (8, LANES), 1) < 64
    row = lax.broadcasted_iota(jnp.int32, (8, LANES), 0)
    for s in range(cap):
        d = got[16 * s:16 * s + 16, :]
        high = d.astype(jnp.bfloat16).astype(jnp.float32)
        low = d - high
        rows = []
        for a in range(4):
            h = pltpu.roll(high, LANES - 32 * a, 1) if a else high
            l = pltpu.roll(low, (LANES + 32 - 32 * a) % LANES, 1) if a != 1 else low
            rows.append(jnp.where(first16, h, l))
        vals[base + s] = jnp.concatenate(rows, axis=0)[:, :64].astype(jnp.bfloat16)
    tiles = []
    for d in range(3):
        start = 16 * cap + (cap // 2) * d
        tile = got[start:start + cap // 2, :]
        turned = pltpu.roll(tile, 64, 1)
        tiles.append((jnp.where(left8, tile, turned), jnp.where(left8, turned, tile)))
    for s in range(cap):
        parts = [jnp.broadcast_to(t[s % 2][s // 2:s // 2 + 1], (8, LANES)) for t in tiles]
        source[base + s] = source_rows(jnp.where(row == 0, parts[0], jnp.where(row == 1, parts[1], parts[2])))


def exchange_kernel(n_grp, n_sub, par, cap, slots,
                    send_list, far_list, own, own_pts, basis, trans, gt, gcoup, coup_hbm,
                    vals, source, target, far,
                    send, recv, ps_all, gs_all, loose_all, field, coup, send_sem, recv_sem, ps_send, ps_recv, gs_send,
                    gs_recv, coup_sem):
    me = lax.axis_index("sub")
    grp = lax.axis_index("grp")
    barrier = pltpu.get_barrier_semaphore()
    for o in range(1, n_sub):
        pl.semaphore_signal(barrier, inc=1, device_id={"sub": lax.rem(me + o, n_sub)}, device_id_type=MESH)
    for o in range(1, n_grp):
        pl.semaphore_signal(barrier, inc=1, device_id={"grp": lax.rem(grp + o, n_grp)}, device_id_type=MESH)

    coup_copy = pltpu.make_async_copy(coup_hbm, coup, coup_sem)
    coup_copy.start()
    left8 = lax.broadcasted_iota(jnp.int32, (8, LANES), 1) < 64

    def pack(peer, carry):
        tops = []
        for s in range(cap):
            leaf = send_list[peer, s]
            block = own[leaf]
            send[peer, 16 * s:16 * s + 16, :] = jnp.concatenate([block[16 * a:16 * a + 16] for a in range(4)], axis=1)
            tops.append(own_pts[leaf])
        for p in range(cap // 2):
            both = jnp.where(left8, tops[2 * p], tops[2 * p + 1])
            for d in range(3):
                row = 16 * cap + (cap // 2) * d + p
                send[peer, row:row + 1, :] = both[d:d + 1]
        return carry

    lax.fori_loop(0, n_sub, pack, 0)
    def value_copy(o):
        peer = lax.rem(me + o, n_sub)
        return pltpu.make_async_remote_copy(
            src_ref=send.at[peer], dst_ref=recv.at[me], send_sem=send_sem.at[o], recv_sem=recv_sem.at[o],
            device_id={"sub": peer}, device_id_type=MESH)

    pl.semaphore_wait(barrier, n_sub - 1 + n_grp - 1)
    early = n_sub // 2
    for o in range(1, early):
        value_copy(o).start()

    same = (lax.broadcasted_iota(jnp.int32, (256, 256), 0) // 32
            == lax.broadcasted_iota(jnp.int32, (256, 256), 1) // 32)

    def lift(c, carry):
        first = pl.multiple_of(c * CHILDREN, CHILDREN)
        rows = pl.ds(pl.multiple_of(c * 256, 256), 256)
        vals = jnp.concatenate([own[first + i] for i in range(CHILDREN)], axis=1)
        skel = jnp.where(same, mm(basis[rows, :], vals), 0.0)
        up = mm(trans[rows, :], skel, ((0,), (0,)))
        y = up[:, :LANES] + up[:, LANES:]
        y = y + pltpu.roll(y, 64, 1)
        y = y + pltpu.roll(y, 32, 1)
        ps_all[me * (par + 1) + c] = dense(y)
        return carry + mm(gt[pl.ds(c, 32, stride=par), :], y)

    part = lax.fori_loop(0, par, lift, jnp.zeros((32, LANES), jnp.float32))
    ps_all[me * (par + 1) + par] = dense(part)

    partner = me + 1 - 2 * lax.rem(me, 2)

    def skel_copy(whose, to, k):
        part = ps_all.at[pl.ds(whose * (par + 1), par + 1)]
        return pltpu.make_async_remote_copy(
            src_ref=part, dst_ref=part, send_sem=ps_send.at[k], recv_sem=ps_recv.at[k],
            device_id={"sub": to}, device_id_type=MESH)

    def direct(o):
        return skel_copy(me, lax.rem(me + o, n_sub), o)

    def forward(o):
        return skel_copy(lax.rem(me + n_sub - o, n_sub), partner, o + 1)

    for o in range(2, n_sub, 2):
        direct(o).start()
    skel_copy(me, partner, 1).start()
    for o in range(early, n_sub):
        value_copy(o).start()

    def keep(l, carry):
        block = own[l]
        high = block.astype(jnp.bfloat16).astype(jnp.float32)
        vals[l] = jnp.concatenate([high, block - high], axis=1).astype(jnp.bfloat16)
        source[l] = source_rows(own_pts[l])
        return carry

    def keep_target(l, carry):
        target[l] = target_columns(own_pts[l])
        return carry

    lax.fori_loop(0, par * CHILDREN, keep, 0, unroll=4)
    vals[slots] = jnp.zeros((64, 64), jnp.bfloat16)
    source[slots] = source_rows(jnp.zeros((8, LANES), jnp.float32))
    for o in range(2, n_sub, 2):
        direct(o).wait_recv()
        forward(o).start()
    lax.fori_loop(0, par * CHILDREN, keep_target, 0, unroll=4)
    unpack(cap, par * CHILDREN + me * cap, send.at[me], vals, source)
    for o in range(2, n_sub, 2):
        direct(o).wait_send()
        forward(o).wait()
    skel_copy(me, partner, 1).wait()

    total = ps_all[par]
    for m in range(1, n_sub):
        total = total + ps_all[m * (par + 1) + par]
    gs_all[grp] = total

    def group_copy(o):
        return pltpu.make_async_remote_copy(
            src_ref=gs_all.at[grp], dst_ref=gs_all.at[grp], send_sem=gs_send.at[o], recv_sem=gs_recv.at[o],
            device_id={"grp": lax.rem(grp + o, n_grp)}, device_id_type=MESH)

    for o in range(1, n_grp):
        group_copy(o).start()

    def loosen(m, carry):
        for c in range(par):
            loose_all[m * par + c] = loose(ps_all[m * (par + 1) + c])
        return carry

    lax.fori_loop(0, n_sub, loosen, 0)
    coup_copy.wait()

    def local(c, carry):
        partners = jnp.concatenate([loose_all[far_list[f, c]] for f in range(16)], axis=0)
        blocks = jnp.concatenate([coup[pl.ds(f * par + c, 32, stride=16 * par), :] for f in range(16)], axis=1)
        field[c] = spread_lanes(mm(blocks, partners))
        return carry

    lax.fori_loop(0, par, local, 0)
    for o in range(1, n_grp):
        group_copy(o).wait()
    inflow = jnp.zeros((32, LANES), jnp.float32)
    for h in range(n_grp):
        live = jnp.where(grp == h, 0.0, 1.0)
        block = gcoup[pl.ds(grp * n_grp + h, 32, stride=n_grp * n_grp), :]
        inflow = inflow + mm(block * live, loose(gs_all[h]))
    inflow = spread_lanes(inflow)

    def down(c, carry):
        rows = pl.ds(pl.multiple_of(c * 256, 256), 256)
        here = field[c] + mm(gt[pl.ds(c, 32, stride=par), :], inflow, ((0,), (0,)))
        leaf_field = mm(here.T, trans[rows, :], ((1,), (1,)))
        spread = jnp.where(same, jnp.concatenate([leaf_field, leaf_field], axis=0), 0.0)
        far[rows, :] = mm(spread, basis[rows, :])
        return carry

    lax.fori_loop(0, par, down, 0)

    def arrive(o, carry):
        value_copy(o).wait_recv()
        sender = lax.rem(me + n_sub - o, n_sub)
        unpack(cap, par * CHILDREN + sender * cap, recv.at[sender], vals, source)
        return carry

    lax.fori_loop(1, n_sub, arrive, 0)
    for o in range(1, n_sub):
        value_copy(o).wait_send()


def near_kernel(leaves, idx, vals, source, target, far, out):
    left48 = lax.broadcasted_iota(jnp.int32, (48, LANES), 1) < 64
    first64 = lax.broadcasted_iota(jnp.int32, (64, 64), 1) < 32

    def some_leaves(step, carry):
        ids = [step * TOGETHER + n for n in range(TOGETHER)]
        entries = [[idx[e, i] for e in range(8)] for i in ids]
        dists = []
        for i, ent in zip(ids, entries):
            points = [jnp.where(left48, source[ent[2 * p]], source[ent[2 * p + 1]]) for p in range(4)]
            dists.append(jnp.dot(target[i], jnp.concatenate(points, axis=1), preferred_element_type=jnp.float32))
        sides = []
        for dist in dists:
            kern = lax.rsqrt(dist)
            high = kern.astype(jnp.bfloat16)
            low = (kern - high.astype(jnp.float32)).astype(jnp.bfloat16)
            sides.append(jnp.concatenate([high, low], axis=0))
        fulls = []
        for ent, side in zip(entries, sides):
            values = jnp.concatenate([vals[e] for e in ent], axis=0)
            fulls.append(jnp.dot(side, values, preferred_element_type=jnp.float32))
        nears = [(full[:64] + jnp.where(first64, full[64:], 0.0)).T for full in fulls]
        for i, near in zip(ids, nears):
            out[i] = far[i] + INV_FOUR_PI * (near[:32] + near[32:])
        return carry

    lax.fori_loop(0, leaves // TOGETHER, some_leaves, 0)


def body(
    sources,
    coords,
    leaf_basis,
    transfer,
    send_list,
    near_list,
    near_count,
    far_list,
    coupling,
    group_transfer,
    group_coupling,
):
    n_sub = lax.axis_size("sub")
    n_grp = lax.axis_size("grp")
    leaves = sources.shape[2]
    par = leaves // CHILDREN
    cap = send_list.shape[1]
    slots = leaves + n_sub * cap
    near_entries = near_list.shape[0]
    f32 = jnp.float32

    own = jnp.transpose(sources, (2, 1, 0))
    y = jnp.transpose(coords, (2, 0, 1))
    own_pts = jnp.pad(jnp.concatenate([y, y], axis=2), ((0, 0), (0, 5), (0, 0)))
    basis = jnp.transpose(leaf_basis, (2, 0, 1)).reshape(leaves * 32, 64)
    trans = jnp.transpose(transfer, (2, 1, 0)).reshape(leaves * 32, 32)
    coup = jnp.transpose(coupling, (0, 2, 3, 1)).reshape(32 * 16 * par, 32)
    gt = jnp.transpose(group_transfer, (0, 2, 1)).reshape(32 * par, 32)
    gcoup = jnp.transpose(group_coupling, (0, 2, 3, 1)).reshape(32 * n_grp * n_grp, 32)
    live = jnp.arange(near_entries, dtype=jnp.int32)[:, None] < near_count[None, :]
    idx = jnp.pad(jnp.where(live, near_list, slots), ((0, 8 - near_entries), (0, 0)), constant_values=slots)

    vmem = pl.BlockSpec(memory_space=pltpu.VMEM)
    smem = pl.BlockSpec(memory_space=pltpu.SMEM)
    rows = 16 * cap + 3 * (cap // 2)
    dma = pltpu.SemaphoreType.DMA
    vals, source, target, far = pl.pallas_call(
        lambda *refs: exchange_kernel(n_grp, n_sub, par, cap, slots, *refs),
        out_shape=(jax.ShapeDtypeStruct((slots + 1, 64, 64), jnp.bfloat16),
                   jax.ShapeDtypeStruct((slots + 1, 48, LANES), jnp.bfloat16),
                   jax.ShapeDtypeStruct((leaves, 64, 48), jnp.bfloat16),
                   jax.ShapeDtypeStruct((leaves * 32, 64), f32)),
        in_specs=[smem, smem] + [vmem] * 6 + [pl.BlockSpec(memory_space=pl.ANY)],
        out_specs=(vmem,) * 4,
        scratch_shapes=[
            pltpu.VMEM((n_sub, rows, LANES), f32),
            pltpu.VMEM((n_sub, rows, LANES), f32),
            pltpu.VMEM((n_sub * (par + 1), 8, LANES), f32),
            pltpu.VMEM((n_grp, 8, LANES), f32),
            pltpu.VMEM((n_sub * par, 32, LANES), f32),
            pltpu.VMEM((par, 32, LANES), f32),
            pltpu.VMEM((32 * 16 * par, 32), f32),
            dma((n_sub,)), dma((n_sub,)), dma((n_sub,)), dma((n_sub,)), dma((n_grp,)), dma((n_grp,)), dma,
        ],
        compiler_params=pltpu.CompilerParams(
            collective_id=0, has_side_effects=True, vmem_limit_bytes=40 * 2**20),
        name="exchange_far",
    )(send_list, far_list, own, own_pts, basis, trans, gt, gcoup, coup)

    out = pl.pallas_call(
        lambda *refs: near_kernel(leaves, *refs),
        out_shape=jax.ShapeDtypeStruct((leaves, 32, 64), f32),
        in_specs=[smem] + [vmem] * 4,
        out_specs=vmem,
        compiler_params=pltpu.CompilerParams(vmem_limit_bytes=32 * 2**20),
        name="near_field",
    )(idx, vals, source, target, far.reshape(leaves, 32, 64))
    return jnp.transpose(out, (1, 2, 0))


def solution(mesh):
    whole = ("grp", "sub")
    return jax.shard_map(
        body,
        mesh=mesh,
        in_specs=(
            P(None, None, whole),
            P(None, None, whole),
            P(None, None, whole),
            P(None, None, whole),
            P(whole, None),
            P(None, whole),
            P(whole),
            P(None, whole),
            P(None, None, None, whole),
            P(None, None, whole),
            P(),
        ),
        out_specs=P(None, None, whole),
        check_vma=False,
    )
```

```python
import math

import jax
import jax.numpy as jnp
from jax import lax
from jax.experimental import pallas as pl
from jax.experimental.pallas import tpu as pltpu
from jax.sharding import PartitionSpec as P

INV_FOUR_PI = 1.0 / (4.0 * math.pi)
EPS_SQ = 0.01
MESH = pl.DeviceIdType.MESH
LANES = 128
CHILDREN = 8
TOGETHER = 4


def halves(x):
    high = x.astype(jnp.bfloat16)
    return high, (x - high.astype(jnp.float32)).astype(jnp.bfloat16)


def mm(a, b, dims=((1,), (0,))):
    def dot(x, y):
        return lax.dot_general(x, y, (dims, ((), ())), preferred_element_type=jnp.float32)
    a0, a1 = halves(a)
    b0, b1 = halves(b)
    return dot(a0, b0) + (dot(a0, b1) + dot(a1, b0))


def lane_block(rows):
    return lax.broadcasted_iota(jnp.int32, (rows, LANES), 1) // 32


def pick_blocks(parts):
    blk = lane_block(parts[0].shape[0])
    out = parts[3]
    for a in (2, 1, 0):
        out = jnp.where(blk == a, parts[a], out)
    return out


def spread_lanes(y):
    y = jnp.where(lane_block(y.shape[0]) == 0, y, 0.0)
    y = y + pltpu.roll(y, 32, 1)
    return y + pltpu.roll(y, 64, 1)


def loose(block):
    return jnp.concatenate([block] + [pltpu.roll(block, LANES - 32 * a, 1) for a in range(1, 4)], axis=0)


def dense(y):
    return pick_blocks([y[8 * a:8 * a + 8] for a in range(4)])


def thirds(x):
    terms = []
    for _ in range(3):
        term = x.astype(jnp.bfloat16).astype(jnp.float32)
        terms.append(term)
        x = x - term
    return terms


def point_rows(tile):
    row = lax.broadcasted_iota(jnp.int32, (8, LANES), 0)
    centred = jnp.where(row < 3, tile - 1.0, 0.0)
    return row, centred, jnp.sum(centred * centred, axis=0, keepdims=True)


def source_rows(tile):
    row, y, norm = point_rows(tile)
    u = thirds(jnp.where(row < 3, y, jnp.where(row == 3, norm, jnp.where(row == 4, 1.0, 0.0))))
    return jnp.concatenate([u[0], u[1], u[0], u[1], u[2], u[0]], axis=0).astype(jnp.bfloat16)


def target_columns(tile):
    row, x, norm = point_rows(tile)
    w = thirds(jnp.where(row < 3, -2.0 * x, jnp.where(row == 3, 1.0, jnp.where(row == 4, norm + EPS_SQ, 0.0))))
    rows = jnp.concatenate([w[0], w[0], w[1], w[1], w[0], w[2]], axis=0)
    return rows.T[:64].astype(jnp.bfloat16)


def value_rows(d):
    first16 = lax.broadcasted_iota(jnp.int32, (16, LANES), 1) < 32
    high = d.astype(jnp.bfloat16).astype(jnp.float32)
    low = d - high
    rows = []
    for a in range(4):
        h = pltpu.roll(high, LANES - 32 * a, 1) if a else high
        l = pltpu.roll(low, (LANES + 32 - 32 * a) % LANES, 1) if a != 1 else low
        rows.append(jnp.where(first16, h, l))
    return jnp.concatenate(rows, axis=0)[:, :64].astype(jnp.bfloat16)


def xor(i, k, size):
    out, bit = 0, 1
    while bit < size:
        x, y = lax.rem(i // bit, 2), lax.rem(k // bit, 2)
        out, bit = out + bit * (x + y - 2 * x * y), 2 * bit
    return out


def unpack(cap, base, got, vals, source):
    left8 = lax.broadcasted_iota(jnp.int32, (8, LANES), 1) < 64
    row = lax.broadcasted_iota(jnp.int32, (8, LANES), 0)
    for s in range(cap):
        vals[base + s] = value_rows(got[16 * s:16 * s + 16, :])
    tiles = []
    for d in range(3):
        start = 16 * cap + (cap // 2) * d
        tile = got[start:start + cap // 2, :]
        turned = pltpu.roll(tile, 64, 1)
        tiles.append((jnp.where(left8, tile, turned), jnp.where(left8, turned, tile)))
    for s in range(cap):
        parts = [jnp.broadcast_to(t[s % 2][s // 2:s // 2 + 1], (8, LANES)) for t in tiles]
        source[base + s] = source_rows(jnp.where(row == 0, parts[0], jnp.where(row == 1, parts[1], parts[2])))


def exchange_kernel(n_grp, n_sub, par, cap, slots,
                    send_list, far_list, src, own_pts, raw_basis, raw_trans, gt, gcoup, coup_hbm,
                    vals, source, target, far,
                    flat, own, basis, trans, send, recv, ps_all, gs_all, loose_all, field, coup, send_sem, recv_sem, ps_send, ps_recv, gs_send,
                    gs_recv, coup_sem):
    me = lax.axis_index("sub")
    grp = lax.axis_index("grp")
    barrier = pltpu.get_barrier_semaphore()
    peers = [me] + [xor(me, k, n_sub) for k in range(1, n_sub)]
    for k in range(1, n_sub):
        pl.semaphore_signal(barrier, inc=1, device_id={"sub": peers[k]}, device_id_type=MESH)
    for o in range(1, n_grp):
        pl.semaphore_signal(barrier, inc=1, device_id={"grp": lax.rem(grp + o, n_grp)}, device_id_type=MESH)

    coup_copy = pltpu.make_async_copy(coup_hbm, coup, coup_sem)
    coup_copy.start()
    leaves = par * CHILDREN

    def turn_sources(q, carry):
        cols = jnp.concatenate([src[pl.ds(16 * a + q, 32, stride=64), :] for a in range(4)], axis=0)
        flat[pl.ds(q, leaves, stride=16), :] = cols.T
        return carry

    def turn_basis(k, carry):
        basis[pl.ds(k, leaves, stride=32), :] = raw_basis[pl.ds(pl.multiple_of(64 * k, 64), 64), :].T
        trans[pl.ds(k, leaves, stride=32), :] = raw_trans[pl.ds(k, 32, stride=32), :].T
        return carry

    def own_copy(l, carry):
        own[l] = flat[pl.ds(pl.multiple_of(16 * l, 16), 16), :]
        return carry

    lax.fori_loop(0, 16, turn_sources, 0, unroll=2)
    lax.fori_loop(0, leaves, own_copy, 0, unroll=16)
    left8 = lax.broadcasted_iota(jnp.int32, (8, LANES), 1) < 64

    def pack(peer, carry):
        tops = []
        for s in range(cap):
            leaf = send_list[peer, s]
            send[peer, 16 * s:16 * s + 16, :] = own[leaf]
            tops.append(own_pts[leaf])
        for p in range(cap // 2):
            both = jnp.where(left8, tops[2 * p], tops[2 * p + 1])
            for d in range(3):
                row = 16 * cap + (cap // 2) * d + p
                send[peer, row:row + 1, :] = both[d:d + 1]
        return carry

    lax.fori_loop(0, n_sub, pack, 0)

    def value_copy(k, peer):
        return pltpu.make_async_remote_copy(
            src_ref=send.at[peer], dst_ref=recv.at[me], send_sem=send_sem.at[k], recv_sem=recv_sem.at[k],
            device_id={"sub": peer}, device_id_type=MESH)

    pl.semaphore_wait(barrier, n_sub - 1 + n_grp - 1)
    half = n_sub // 2
    for k in (half, 1):
        value_copy(k, peers[k]).start()
    lax.fori_loop(0, 32, turn_basis, 0, unroll=2)

    same = (lax.broadcasted_iota(jnp.int32, (256, 256), 0) // 32
            == lax.broadcasted_iota(jnp.int32, (256, 256), 1) // 32)

    def lift(c, carry):
        first = pl.multiple_of(c * CHILDREN, CHILDREN)
        rows = pl.ds(pl.multiple_of(c * 256, 256), 256)
        sides = []
        for side in range(2):
            four = [own[first + 4 * side + i] for i in range(4)]
            sides.append(jnp.concatenate([
                pick_blocks([pltpu.roll(x, 32 * (i - a) % LANES, 1) if i != a else x for i, x in enumerate(four)])
                for a in range(4)], axis=0))
        skel = jnp.where(same, mm(basis[rows, :], jnp.concatenate(sides, axis=1)), 0.0)
        up = mm(trans[rows, :], skel, ((0,), (0,)))
        y = up[:, :LANES] + up[:, LANES:]
        y = y + pltpu.roll(y, 64, 1)
        y = y + pltpu.roll(y, 32, 1)
        ps_all[me * (par + 1) + c] = dense(y)
        return carry + mm(gt[pl.ds(c, 32, stride=par), :], y)

    part = lax.fori_loop(0, par, lift, jnp.zeros((32, LANES), jnp.float32))
    ps_all[me * (par + 1) + par] = dense(part)

    def skel_copy(whose, to, k):
        part = ps_all.at[pl.ds(whose * (par + 1), par + 1)]
        return pltpu.make_async_remote_copy(
            src_ref=part, dst_ref=part, send_sem=ps_send.at[k], recv_sem=ps_recv.at[k],
            device_id={"sub": to}, device_id_type=MESH)

    def direct(k):
        return skel_copy(me, peers[k], k)

    def forward(k):
        return skel_copy(peers[k], peers[1], k + 1)

    evens = range(n_sub - 2, 0, -2)
    for k in evens:
        direct(k).start()
    direct(1).start()

    def keep(l, carry):
        vals[l] = value_rows(own[l])
        source[l] = source_rows(own_pts[l])
        return carry

    def keep_target(l, carry):
        target[l] = target_columns(own_pts[l])
        return carry

    lax.fori_loop(0, leaves, keep, 0, unroll=8)
    for k in evens:
        direct(k).wait_recv()
        forward(k).start()
    for k in list(range(half + 1, n_sub)) + list(range(2, half)):
        value_copy(k, peers[k]).start()
    vals[slots] = jnp.zeros((64, 64), jnp.bfloat16)
    source[slots] = source_rows(jnp.zeros((8, LANES), jnp.float32))
    lax.fori_loop(0, leaves, keep_target, 0, unroll=8)
    unpack(cap, leaves + me * cap, send.at[me], vals, source)
    for k in evens:
        direct(k).wait_send()
        forward(k).wait()
    direct(1).wait()

    total = ps_all[par]
    for m in range(1, n_sub):
        total = total + ps_all[m * (par + 1) + par]
    gs_all[grp] = total

    def group_copy(o):
        return pltpu.make_async_remote_copy(
            src_ref=gs_all.at[grp], dst_ref=gs_all.at[grp], send_sem=gs_send.at[o], recv_sem=gs_recv.at[o],
            device_id={"grp": lax.rem(grp + o, n_grp)}, device_id_type=MESH)

    for o in range(1, n_grp):
        group_copy(o).start()

    def loosen(m, carry):
        for c in range(par):
            loose_all[m * par + c] = loose(ps_all[m * (par + 1) + c])
        return carry

    lax.fori_loop(0, n_sub, loosen, 0)
    coup_copy.wait()

    def local(c, carry):
        partners = jnp.concatenate([loose_all[far_list[f, c]] for f in range(16)], axis=0)
        blocks = jnp.concatenate([coup[pl.ds(f * par + c, 32, stride=16 * par), :] for f in range(16)], axis=1)
        field[c] = spread_lanes(mm(blocks, partners))
        return carry

    lax.fori_loop(0, par, local, 0)
    for o in range(1, n_grp):
        group_copy(o).wait()
    inflow = jnp.zeros((32, LANES), jnp.float32)
    for h in range(n_grp):
        live = jnp.where(grp == h, 0.0, 1.0)
        block = gcoup[pl.ds(grp * n_grp + h, 32, stride=n_grp * n_grp), :]
        inflow = inflow + mm(block * live, loose(gs_all[h]))
    inflow = spread_lanes(inflow)

    def down(c, carry):
        rows = pl.ds(pl.multiple_of(c * 256, 256), 256)
        here = field[c] + mm(gt[pl.ds(c, 32, stride=par), :], inflow, ((0,), (0,)))
        leaf_field = mm(here.T, trans[rows, :], ((1,), (1,)))
        spread = jnp.where(same, jnp.concatenate([leaf_field, leaf_field], axis=0), 0.0)
        far[rows, :] = mm(spread, basis[rows, :])
        return carry

    lax.fori_loop(0, par, down, 0)

    def arrive(k, carry):
        peer = xor(me, k, n_sub)
        value_copy(k, peer).wait_recv()
        unpack(cap, leaves + peer * cap, recv.at[peer], vals, source)
        return carry

    arrive(1, 0)
    lax.fori_loop(half, n_sub, arrive, 0)
    lax.fori_loop(2, half, arrive, 0)
    for k in range(1, n_sub):
        value_copy(k, peers[k]).wait_send()


def near_kernel(leaves, idx, vals, source, target, far, out):
    left48 = lax.broadcasted_iota(jnp.int32, (48, LANES), 1) < 64
    first64 = lax.broadcasted_iota(jnp.int32, (64, 64), 1) < 32

    def some_leaves(step, carry):
        ids = [step * TOGETHER + n for n in range(TOGETHER)]
        entries = [[idx[e, i] for e in range(8)] for i in ids]
        dists = []
        for i, ent in zip(ids, entries):
            points = [jnp.where(left48, source[ent[2 * p]], source[ent[2 * p + 1]]) for p in range(4)]
            dists.append(jnp.dot(target[i], jnp.concatenate(points, axis=1), preferred_element_type=jnp.float32))
        sides = []
        for dist in dists:
            kern = lax.rsqrt(dist)
            high = kern.astype(jnp.bfloat16)
            low = (kern - high.astype(jnp.float32)).astype(jnp.bfloat16)
            sides.append(jnp.concatenate([high, low], axis=0))
        fulls = []
        for ent, side in zip(entries, sides):
            values = jnp.concatenate([vals[e] for e in ent], axis=0)
            fulls.append(jnp.dot(side, values, preferred_element_type=jnp.float32))
        nears = [(full[:64] + jnp.where(first64, full[64:], 0.0)).T for full in fulls]
        for i, near in zip(ids, nears):
            out[i] = far[i] + INV_FOUR_PI * (near[:32] + near[32:])
        return carry

    lax.fori_loop(0, leaves // TOGETHER, some_leaves, 0)


def body(
    sources,
    coords,
    leaf_basis,
    transfer,
    send_list,
    near_list,
    near_count,
    far_list,
    coupling,
    group_transfer,
    group_coupling,
):
    n_sub = lax.axis_size("sub")
    n_grp = lax.axis_size("grp")
    leaves = sources.shape[2]
    par = leaves // CHILDREN
    cap = send_list.shape[1]
    slots = leaves + n_sub * cap
    near_entries = near_list.shape[0]
    f32 = jnp.float32

    y = jnp.transpose(coords, (2, 0, 1))
    own_pts = jnp.pad(jnp.concatenate([y, y], axis=2), ((0, 0), (0, 5), (0, 0)))
    coup = jnp.transpose(coupling, (0, 2, 3, 1)).reshape(32 * 16 * par, 32)
    gt = jnp.transpose(group_transfer, (0, 2, 1)).reshape(32 * par, 32)
    gcoup = jnp.transpose(group_coupling, (0, 2, 3, 1)).reshape(32 * n_grp * n_grp, 32)
    live = jnp.arange(near_entries, dtype=jnp.int32)[:, None] < near_count[None, :]
    idx = jnp.pad(jnp.where(live, near_list, slots), ((0, 8 - near_entries), (0, 0)), constant_values=slots)

    vmem = pl.BlockSpec(memory_space=pltpu.VMEM)
    smem = pl.BlockSpec(memory_space=pltpu.SMEM)
    rows = 16 * cap + 3 * (cap // 2)
    dma = pltpu.SemaphoreType.DMA
    vals, source, target, far = pl.pallas_call(
        lambda *refs: exchange_kernel(n_grp, n_sub, par, cap, slots, *refs),
        out_shape=(jax.ShapeDtypeStruct((slots + 1, 64, 64), jnp.bfloat16),
                   jax.ShapeDtypeStruct((slots + 1, 48, LANES), jnp.bfloat16),
                   jax.ShapeDtypeStruct((leaves, 64, 48), jnp.bfloat16),
                   jax.ShapeDtypeStruct((leaves * 32, 64), f32)),
        in_specs=[smem, smem] + [vmem] * 6 + [pl.BlockSpec(memory_space=pl.ANY)],
        out_specs=(vmem,) * 4,
        scratch_shapes=[
            pltpu.VMEM((leaves * 16, LANES), f32),
            pltpu.VMEM((leaves, 16, LANES), f32),
            pltpu.VMEM((leaves * 32, 64), f32),
            pltpu.VMEM((leaves * 32, 32), f32),
            pltpu.VMEM((n_sub, rows, LANES), f32),
            pltpu.VMEM((n_sub, rows, LANES), f32),
            pltpu.VMEM((n_sub * (par + 1), 8, LANES), f32),
            pltpu.VMEM((n_grp, 8, LANES), f32),
            pltpu.VMEM((n_sub * par, 32, LANES), f32),
            pltpu.VMEM((par, 32, LANES), f32),
            pltpu.VMEM((32 * 16 * par, 32), f32),
            dma((n_sub,)), dma((n_sub,)), dma((n_sub,)), dma((n_sub,)), dma((n_grp,)), dma((n_grp,)), dma,
        ],
        compiler_params=pltpu.CompilerParams(
            collective_id=0, has_side_effects=True, vmem_limit_bytes=34 * 2**20),
        name="exchange_far",
    )(send_list, far_list, sources.reshape(32 * 64, leaves), own_pts, leaf_basis.reshape(32 * 64, leaves),
      transfer.reshape(32 * 32, leaves), gt, gcoup, coup)

    out = pl.pallas_call(
        lambda *refs: near_kernel(leaves, *refs),
        out_shape=jax.ShapeDtypeStruct((leaves, 32, 64), f32),
        in_specs=[smem] + [vmem] * 4,
        out_specs=vmem,
        compiler_params=pltpu.CompilerParams(vmem_limit_bytes=20 * 2**20),
        name="near_field",
    )(idx, vals, source, target, far.reshape(leaves, 32, 64))
    return jnp.transpose(out, (1, 2, 0))


def solution(mesh):
    whole = ("grp", "sub")
    return jax.shard_map(
        body,
        mesh=mesh,
        in_specs=(
            P(None, None, whole),
            P(None, None, whole),
            P(None, None, whole),
            P(None, None, whole),
            P(whole, None),
            P(None, whole),
            P(whole),
            P(None, whole),
            P(None, None, None, whole),
            P(None, None, whole),
            P(),
        ),
        out_specs=P(None, None, whole),
        check_vma=False,
    )
```

```python
import math

import jax
import jax.numpy as jnp
from jax import lax
from jax.experimental import pallas as pl
from jax.experimental.pallas import tpu as pltpu
from jax.sharding import PartitionSpec as P

INV_FOUR_PI = 1.0 / (4.0 * math.pi)
EPS_SQ = 0.01
MESH = pl.DeviceIdType.MESH
LANES = 128
CHILDREN = 8
TOGETHER = 8
STAGE = 4


def halves(x):
    high = x.astype(jnp.bfloat16)
    return high, (x - high.astype(jnp.float32)).astype(jnp.bfloat16)


def mm(a, b, dims=((1,), (0,))):
    def dot(x, y):
        return lax.dot_general(x, y, (dims, ((), ())), preferred_element_type=jnp.float32)
    a0, a1 = halves(a)
    b0, b1 = halves(b)
    return dot(a0, b0) + (dot(a0, b1) + dot(a1, b0))


def lane_block(rows):
    return lax.broadcasted_iota(jnp.int32, (rows, LANES), 1) // 32


def pick_blocks(parts):
    blk = lane_block(parts[0].shape[0])
    out = parts[3]
    for a in (2, 1, 0):
        out = jnp.where(blk == a, parts[a], out)
    return out


def spread_lanes(y):
    y = jnp.where(lane_block(y.shape[0]) == 0, y, 0.0)
    y = y + pltpu.roll(y, 32, 1)
    return y + pltpu.roll(y, 64, 1)


def loose(block):
    return jnp.concatenate([block] + [pltpu.roll(block, LANES - 32 * a, 1) for a in range(1, 4)], axis=0)


def dense(y):
    return pick_blocks([y[8 * a:8 * a + 8] for a in range(4)])


def thirds(x):
    terms = []
    for _ in range(3):
        term = x.astype(jnp.bfloat16).astype(jnp.float32)
        terms.append(term)
        x = x - term
    return terms


def point_rows(tile):
    row = lax.broadcasted_iota(jnp.int32, (8, LANES), 0)
    centred = jnp.where(row < 3, tile - 1.0, 0.0)
    return row, centred, jnp.sum(centred * centred, axis=0, keepdims=True)


def source_rows(tile):
    row, y, norm = point_rows(tile)
    u = thirds(jnp.where(row < 3, y, jnp.where(row == 3, norm, jnp.where(row == 4, 1.0, 0.0))))
    return jnp.concatenate([u[0], u[1], u[0], u[1], u[2], u[0]], axis=0).astype(jnp.bfloat16)


def target_columns(tile):
    row, x, norm = point_rows(tile)
    w = thirds(jnp.where(row < 3, -2.0 * x, jnp.where(row == 3, 1.0, jnp.where(row == 4, norm + EPS_SQ, 0.0))))
    rows = jnp.concatenate([w[0], w[0], w[1], w[1], w[0], w[2]], axis=0)
    return rows.T[:64].astype(jnp.bfloat16)


def value_rows(d):
    first16 = lax.broadcasted_iota(jnp.int32, (16, LANES), 1) < 32
    high = d.astype(jnp.bfloat16).astype(jnp.float32)
    low = d - high
    rows = []
    for a in range(4):
        h = pltpu.roll(high, LANES - 32 * a, 1) if a else high
        l = pltpu.roll(low, (LANES + 32 - 32 * a) % LANES, 1) if a != 1 else low
        rows.append(jnp.where(first16, h, l))
    return jnp.concatenate(rows, axis=0)[:, :64].astype(jnp.bfloat16)


def xor(i, k, size):
    out, bit = 0, 1
    while bit < size:
        x, y = lax.rem(i // bit, 2), lax.rem(k // bit, 2)
        out, bit = out + bit * (x + y - 2 * x * y), 2 * bit
    return out


def unpack(cap, base, got, vals, source):
    left8 = lax.broadcasted_iota(jnp.int32, (8, LANES), 1) < 64
    row = lax.broadcasted_iota(jnp.int32, (8, LANES), 0)
    tables = [value_rows(got[16 * s:16 * s + 16, :]) for s in range(cap)]
    for s in range(cap):
        vals[base + s] = tables[s]
    tiles = []
    for d in range(3):
        start = 16 * cap + (cap // 2) * d
        tile = got[start:start + cap // 2, :]
        turned = pltpu.roll(tile, 64, 1)
        tiles.append((jnp.where(left8, tile, turned), jnp.where(left8, turned, tile)))
    tables = []
    for s in range(cap):
        parts = [jnp.broadcast_to(t[s % 2][s // 2:s // 2 + 1], (8, LANES)) for t in tiles]
        tables.append(source_rows(jnp.where(row == 0, parts[0], jnp.where(row == 1, parts[1], parts[2]))))
    for s in range(cap):
        source[base + s] = tables[s]


def exchange_kernel(n_grp, n_sub, par, cap, slots,
                    send_list, far_list, idx, own_pts, src_hbm, basis_hbm, trans_hbm, gt_hbm, gcoup_hbm, coup_hbm,
                    out,
                    vals, source, target, far, src, raw_basis, raw_trans, gt, gcoup, flat, own, basis, trans, send, recv, ps_all, gs_all, loose_all, field, coup, send_sem, recv_sem, ps_send, ps_recv, gs_send,
                    gs_recv, load_sem):
    me = lax.axis_index("sub")
    grp = lax.axis_index("grp")
    barrier = pltpu.get_barrier_semaphore()
    peers = [me] + [xor(me, k, n_sub) for k in range(1, n_sub)]
    for k in range(1, n_sub):
        pl.semaphore_signal(barrier, inc=1, device_id={"sub": peers[k]}, device_id_type=MESH)
    for o in range(1, n_grp):
        pl.semaphore_signal(barrier, inc=1, device_id={"grp": lax.rem(grp + o, n_grp)}, device_id_type=MESH)

    loads = [pltpu.make_async_copy(there, here, load_sem.at[n]) for n, (there, here) in enumerate([
        (src_hbm, src), (basis_hbm, raw_basis), (trans_hbm, raw_trans), (gt_hbm, gt), (gcoup_hbm, gcoup),
        (coup_hbm, coup)])]
    for load in loads:
        load.start()
    leaves = par * CHILDREN

    def turn_sources(step, carry):
        qs = [STAGE * step + n for n in range(STAGE)]
        cols = [jnp.concatenate([src[pl.ds(16 * a + q, 32, stride=64), :] for a in range(4)], axis=0).T for q in qs]
        for q, col in zip(qs, cols):
            flat[pl.ds(q, leaves, stride=16), :] = col
        return carry

    def turn_basis(step, carry):
        ks = [STAGE * step + n for n in range(STAGE)]
        turned = [raw_basis[pl.ds(pl.multiple_of(64 * k, 64), 64), :].T for k in ks]
        moved = [raw_trans[pl.ds(k, 32, stride=32), :].T for k in ks]
        for k, b, t in zip(ks, turned, moved):
            basis[pl.ds(k, leaves, stride=32), :] = b
            trans[pl.ds(k, leaves, stride=32), :] = t
        return carry

    def own_copy(step, carry):
        rows = flat[pl.ds(pl.multiple_of(256 * step, 256), 256), :]
        own[pl.ds(pl.multiple_of(16 * step, 16), 16)] = rows.reshape(16, 16, LANES)
        return carry

    loads[0].wait()
    lax.fori_loop(0, 16 // STAGE, turn_sources, 0)
    lax.fori_loop(0, leaves // 16, own_copy, 0)
    left8 = lax.broadcasted_iota(jnp.int32, (8, LANES), 1) < 64

    def pack(peer, carry):
        chosen = [send_list[peer, s] for s in range(cap)]
        blocks = [own[leaf] for leaf in chosen]
        tops = [own_pts[leaf] for leaf in chosen]
        for s in range(cap):
            send[peer, 16 * s:16 * s + 16, :] = blocks[s]
        for p in range(cap // 2):
            both = jnp.where(left8, tops[2 * p], tops[2 * p + 1])
            for d in range(3):
                row = 16 * cap + (cap // 2) * d + p
                send[peer, row:row + 1, :] = both[d:d + 1]
        return carry

    lax.fori_loop(0, n_sub, pack, 0)

    def value_copy(k, peer):
        return pltpu.make_async_remote_copy(
            src_ref=send.at[peer], dst_ref=recv.at[me], send_sem=send_sem.at[k], recv_sem=recv_sem.at[k],
            device_id={"sub": peer}, device_id_type=MESH)

    pl.semaphore_wait(barrier, n_sub - 1 + n_grp - 1)
    half = n_sub // 2
    for k in (half, 1):
        value_copy(k, peers[k]).start()
    for load in loads[1:4]:
        load.wait()
    lax.fori_loop(0, 32 // STAGE, turn_basis, 0)

    same = (lax.broadcasted_iota(jnp.int32, (256, 256), 0) // 32
            == lax.broadcasted_iota(jnp.int32, (256, 256), 1) // 32)

    def rows_of(c):
        return pl.ds(pl.multiple_of(c * 256, 256), 256)

    def columns(c):
        sides = []
        for side in range(2):
            four = [own[c * CHILDREN + 4 * side + i] for i in range(4)]
            sides.append(jnp.concatenate([
                pick_blocks([pltpu.roll(x, 32 * (i - a) % LANES, 1) if i != a else x for i, x in enumerate(four)])
                for a in range(4)], axis=0))
        return jnp.concatenate(sides, axis=1)

    def lift(step, carry):
        cs = [STAGE * step + n for n in range(STAGE)]
        sides = [columns(c) for c in cs]
        skels = [jnp.where(same, mm(basis[rows_of(c), :], v), 0.0) for c, v in zip(cs, sides)]
        ups = [mm(trans[rows_of(c), :], skel, ((0,), (0,))) for c, skel in zip(cs, skels)]
        ys = [up[:, :LANES] + up[:, LANES:] for up in ups]
        ys = [y + pltpu.roll(y, 64, 1) for y in ys]
        ys = [y + pltpu.roll(y, 32, 1) for y in ys]
        parts = [mm(gt[pl.ds(c, 32, stride=par), :], y) for c, y in zip(cs, ys)]
        for c, y in zip(cs, ys):
            ps_all[me * (par + 1) + c] = dense(y)
        return carry + sum(parts)

    part = lax.fori_loop(0, par // STAGE, lift, jnp.zeros((32, LANES), jnp.float32))
    ps_all[me * (par + 1) + par] = dense(part)

    def skel_copy(whose, to, k):
        part = ps_all.at[pl.ds(whose * (par + 1), par + 1)]
        return pltpu.make_async_remote_copy(
            src_ref=part, dst_ref=part, send_sem=ps_send.at[k], recv_sem=ps_recv.at[k],
            device_id={"sub": to}, device_id_type=MESH)

    def direct(k):
        return skel_copy(me, peers[k], k)

    def forward(k):
        return skel_copy(peers[k], peers[1], k + 1)

    evens = range(n_sub - 2, 0, -2)
    for k in evens:
        direct(k).start()
    direct(1).start()

    def keep(step, carry):
        ls = [8 * step + n for n in range(8)]
        values = [value_rows(own[l]) for l in ls]
        points = [source_rows(own_pts[l]) for l in ls]
        for l, v, p in zip(ls, values, points):
            vals[l] = v
            source[l] = p
        return carry

    def keep_target(step, carry):
        ls = [8 * step + n for n in range(8)]
        points = [target_columns(own_pts[l]) for l in ls]
        for l, p in zip(ls, points):
            target[l] = p
        return carry

    lax.fori_loop(0, leaves // 8, keep, 0)
    for k in evens:
        direct(k).wait_recv()
        forward(k).start()
    for k in list(range(half + 1, n_sub)) + list(range(2, half)):
        value_copy(k, peers[k]).start()
    vals[slots] = jnp.zeros((64, 64), jnp.bfloat16)
    source[slots] = source_rows(jnp.zeros((8, LANES), jnp.float32))
    lax.fori_loop(0, leaves // 8, keep_target, 0)
    unpack(cap, leaves + me * cap, send.at[me], vals, source)
    for k in evens:
        direct(k).wait_send()
        forward(k).wait()
    direct(1).wait()

    total = ps_all[par]
    for m in range(1, n_sub):
        total = total + ps_all[m * (par + 1) + par]
    gs_all[grp] = total

    def group_copy(o):
        return pltpu.make_async_remote_copy(
            src_ref=gs_all.at[grp], dst_ref=gs_all.at[grp], send_sem=gs_send.at[o], recv_sem=gs_recv.at[o],
            device_id={"grp": lax.rem(grp + o, n_grp)}, device_id_type=MESH)

    for o in range(1, n_grp):
        group_copy(o).start()

    def loosen(m, carry):
        for c in range(par):
            loose_all[m * par + c] = loose(ps_all[m * (par + 1) + c])
        return carry

    lax.fori_loop(0, n_sub, loosen, 0)
    for load in loads[4:]:
        load.wait()

    def local(step, carry):
        cs = [STAGE * step + n for n in range(STAGE)]
        sums = []
        for c in cs:
            partners = jnp.concatenate([loose_all[far_list[f, c]] for f in range(16)], axis=0)
            blocks = jnp.concatenate([coup[pl.ds(f * par + c, 32, stride=16 * par), :] for f in range(16)], axis=1)
            sums.append(mm(blocks, partners))
        sums = [spread_lanes(x) for x in sums]
        for c, x in zip(cs, sums):
            field[c] = x
        return carry

    lax.fori_loop(0, par // STAGE, local, 0)
    for o in range(1, n_grp):
        group_copy(o).wait()
    inflow = jnp.zeros((32, LANES), jnp.float32)
    for h in range(n_grp):
        live = jnp.where(grp == h, 0.0, 1.0)
        block = gcoup[pl.ds(grp * n_grp + h, 32, stride=n_grp * n_grp), :]
        inflow = inflow + mm(block * live, loose(gs_all[h]))
    inflow = spread_lanes(inflow)

    def down(step, carry):
        cs = [STAGE * step + n for n in range(STAGE)]
        here = [(field[c] + mm(gt[pl.ds(c, 32, stride=par), :], inflow, ((0,), (0,)))).T for c in cs]
        leaf_fields = [mm(x, trans[rows_of(c), :], ((1,), (1,))) for c, x in zip(cs, here)]
        spreads = [jnp.where(same, jnp.concatenate([x, x], axis=0), 0.0) for x in leaf_fields]
        results = [mm(x, basis[rows_of(c), :]) for c, x in zip(cs, spreads)]
        for c, x in zip(cs, results):
            far[rows_of(c), :] = x
        return carry

    lax.fori_loop(0, par // STAGE, down, 0)

    def arrive(k, carry):
        peer = xor(me, k, n_sub)
        value_copy(k, peer).wait_recv()
        unpack(cap, leaves + peer * cap, recv.at[peer], vals, source)
        return carry

    arrive(1, 0)
    lax.fori_loop(half, n_sub, arrive, 0)
    lax.fori_loop(2, half, arrive, 0)
    for k in range(1, n_sub):
        value_copy(k, peers[k]).wait_send()
    near_field(leaves, idx, vals, source, target, far, out)


def near_field(leaves, idx, vals, source, target, far, out):
    left48 = lax.broadcasted_iota(jnp.int32, (48, LANES), 1) < 64
    first64 = lax.broadcasted_iota(jnp.int32, (64, 64), 1) < 32

    def some_leaves(step, carry):
        ids = [step * TOGETHER + n for n in range(TOGETHER)]
        entries = [[idx[e, i] for e in range(8)] for i in ids]
        dists = []
        for i, ent in zip(ids, entries):
            points = [jnp.where(left48, source[ent[2 * p]], source[ent[2 * p + 1]]) for p in range(4)]
            dists.append(jnp.dot(target[i], jnp.concatenate(points, axis=1), preferred_element_type=jnp.float32))
        sides = []
        for dist in dists:
            kern = lax.rsqrt(dist)
            high = kern.astype(jnp.bfloat16)
            low = (kern - high.astype(jnp.float32)).astype(jnp.bfloat16)
            sides.append(jnp.concatenate([high, low], axis=0))
        fulls = []
        for ent, side in zip(entries, sides):
            values = jnp.concatenate([vals[e] for e in ent], axis=0)
            fulls.append(jnp.dot(side, values, preferred_element_type=jnp.float32))
        nears = [(full[:64] + jnp.where(first64, full[64:], 0.0)).T for full in fulls]
        for i, near in zip(ids, nears):
            out[i] = far[pl.ds(pl.multiple_of(32 * i, 32), 32), :] + INV_FOUR_PI * (near[:32] + near[32:])
        return carry

    lax.fori_loop(0, leaves // TOGETHER, some_leaves, 0)


def body(
    sources,
    coords,
    leaf_basis,
    transfer,
    send_list,
    near_list,
    near_count,
    far_list,
    coupling,
    group_transfer,
    group_coupling,
):
    n_sub = lax.axis_size("sub")
    n_grp = lax.axis_size("grp")
    leaves = sources.shape[2]
    par = leaves // CHILDREN
    cap = send_list.shape[1]
    slots = leaves + n_sub * cap
    near_entries = near_list.shape[0]
    f32 = jnp.float32

    y = jnp.transpose(coords, (2, 0, 1))
    own_pts = jnp.pad(jnp.concatenate([y, y], axis=2), ((0, 0), (0, 5), (0, 0)))
    coup = jnp.transpose(coupling, (0, 2, 3, 1)).reshape(32 * 16 * par, 32)
    gt = jnp.transpose(group_transfer, (0, 2, 1)).reshape(32 * par, 32)
    gcoup = jnp.transpose(group_coupling, (0, 2, 3, 1)).reshape(32 * n_grp * n_grp, 32)
    live = jnp.arange(near_entries, dtype=jnp.int32)[:, None] < near_count[None, :]
    idx = jnp.pad(jnp.where(live, near_list, slots), ((0, 8 - near_entries), (0, 0)), constant_values=slots)

    vmem = pl.BlockSpec(memory_space=pltpu.VMEM)
    smem = pl.BlockSpec(memory_space=pltpu.SMEM)
    rows = 16 * cap + 3 * (cap // 2)
    dma = pltpu.SemaphoreType.DMA
    out = pl.pallas_call(
        lambda *refs: exchange_kernel(n_grp, n_sub, par, cap, slots, *refs),
        out_shape=jax.ShapeDtypeStruct((leaves, 32, 64), f32),
        in_specs=[smem, smem, smem, vmem] + [pl.BlockSpec(memory_space=pltpu.HBM)] * 6,
        out_specs=vmem,
        scratch_shapes=[
            pltpu.VMEM((slots + 1, 64, 64), jnp.bfloat16),
            pltpu.VMEM((slots + 1, 48, LANES), jnp.bfloat16),
            pltpu.VMEM((leaves, 64, 48), jnp.bfloat16),
            pltpu.VMEM((leaves * 32, 64), f32),
            pltpu.VMEM((32 * 64, leaves), f32),
            pltpu.VMEM((32 * 64, leaves), f32),
            pltpu.VMEM((32 * 32, leaves), f32),
            pltpu.VMEM((32 * par, 32), f32),
            pltpu.VMEM((32 * n_grp * n_grp, 32), f32),
            pltpu.VMEM((leaves * 16, LANES), f32),
            pltpu.VMEM((leaves, 16, LANES), f32),
            pltpu.VMEM((leaves * 32, 64), f32),
            pltpu.VMEM((leaves * 32, 32), f32),
            pltpu.VMEM((n_sub, rows, LANES), f32),
            pltpu.VMEM((n_sub, rows, LANES), f32),
            pltpu.VMEM((n_sub * (par + 1), 8, LANES), f32),
            pltpu.VMEM((n_grp, 8, LANES), f32),
            pltpu.VMEM((n_sub * par, 32, LANES), f32),
            pltpu.VMEM((par, 32, LANES), f32),
            pltpu.VMEM((32 * 16 * par, 32), f32),
            dma((n_sub,)), dma((n_sub,)), dma((n_sub,)), dma((n_sub,)), dma((n_grp,)), dma((n_grp,)), dma((6,)),
        ],
        compiler_params=pltpu.CompilerParams(
            collective_id=0, has_side_effects=True, vmem_limit_bytes=56 * 2**20),
        name="whole_step",
    )(send_list, far_list, idx, own_pts, sources.reshape(32 * 64, leaves), leaf_basis.reshape(32 * 64, leaves),
      transfer.reshape(32 * 32, leaves), gt, gcoup, coup)

    return jnp.transpose(out, (1, 2, 0))


def solution(mesh):
    whole = ("grp", "sub")
    return jax.shard_map(
        body,
        mesh=mesh,
        in_specs=(
            P(None, None, whole),
            P(None, None, whole),
            P(None, None, whole),
            P(None, None, whole),
            P(whole, None),
            P(None, whole),
            P(whole),
            P(None, whole),
            P(None, None, None, whole),
            P(None, None, whole),
            P(),
        ),
        out_specs=P(None, None, whole),
        check_vma=False,
    )
```
